32 devices in a mesh: ckpt: 2 (over x), train: 16 (over z, y, core).
Axes of the slice: x: 2, y: 2, z: 4, core: 2. Of those that a mesh axis runs over, the one named last changes fastest.
Arguments:
- train_feat: bfloat16 [2, 32768, 1024], P('ckpt', 'train'), may hold values from -6 to 6
- test_feat: bfloat16 [2, 1024, 1024], P('ckpt', 'train'), may hold values from -0.375 to 0.375
- kernel_inv: bfloat16 [2, 1024, 1024], P('ckpt', 'train'), may hold values from -0.1875 to 0.1875
- bucket_weight: float32 [2, 16], P('ckpt'), may hold values from 0.2 to 2
- bucket: int32 [32768], P('train'), may hold values from 0 to 15
- test_order: int32 [1024], replicated, may hold values from 0 to 1023, each once
Outputs:
- scores: float32 [32768, 1024], P('train', 'ckpt')
The draws below stay inside these ranges and needn't reach their ends.
Inputs may be any that keep to these rules, and one draw needn't show every extreme that they name: `test_order`: each of 0 to 1023 once.
All inputs are finite; a program needn't handle non-finite values.
Results may differ from the reference program's by a relative error of at most 0.012.
Values may be sent and summed in bfloat16 or wider, within the bound.
No kernel may reach another device: no remote copies, remote signals or barrier semaphores. Data moves between devices by JAX's collectives and lax.ppermute only.
A program may use at most 64 MiB of HBM per device.

```python
import math
import jax
import jax.numpy as jnp
from jax import lax

P_SIZE = 1024
NTEST = 1024
NB = 16
CK_DEV = 1
K = 2
NTRAIN = 32768
N_CKPT = 2


def with_ends(entries, key, low, high):
    extent = entries.shape
    index_at = [jax.random.randint(jax.random.fold_in(key, axis), (), 0, extent[axis]) for axis in range(len(extent))]
    entries = entries.at[tuple(index_at)].set(low)
    longest = extent.index(max(extent))
    index_at[longest] = (index_at[longest] + 1) % extent[longest]
    return entries.at[tuple(index_at)].set(high)


def levels(stream_key, shape, pieces, low, largest):
    gain, own = 1.0, jax.random.fold_in(stream_key, 6)
    for dim, parts in pieces:
        steps = jnp.exp(jax.random.uniform(jax.random.fold_in(own, dim), (parts,), jnp.float32, low / len(pieces), largest / len(pieces)))
        gain = gain * jnp.repeat(steps, shape[dim] // parts).reshape([-1 if axis == dim else 1 for axis in range(len(shape))])
    return gain


def noise(own_key, shape, deviation, reach, shards=(), dtype=jnp.bfloat16):
    gain = levels(own_key, shape, shards, -0.22, 0.18) if shards else 1.0
    array = jax.random.normal(own_key, shape, jnp.float32) * deviation * gain
    return jnp.minimum(jnp.maximum(array, -reach), reach).astype(dtype)


def setup_inputs(seed: int = 0) -> dict:
    streams_of = jax.random.split(jax.random.key(seed), 7)
    return {
        "train_feat": noise(streams_of[0], (K, NTRAIN, P_SIZE), 1.0, 6.0, ((0, 2), (1, 16))),
        "test_feat": noise(streams_of[1], (K, NTEST, P_SIZE), 0.0625, 0.375, ((0, 2), (1, 16))),
        "kernel_inv": noise(streams_of[2], (K, P_SIZE, P_SIZE), P_SIZE ** -0.5, 0.1875, ((0, 2), (1, 16))),
        "bucket_weight": jnp.clip(jnp.exp(math.log(2.0) - 2.3025851 * jax.random.uniform(streams_of[3], (K, NB), jnp.float32) ** levels(streams_of[3], (K, NB), ((0, 2),), -0.2, 0.2)), 0.2, 2.0),
        "bucket": with_ends(jax.random.randint(streams_of[4], (NTRAIN,), 0, NB), jax.random.fold_in(streams_of[4], 1), 0, NB - 1).astype(jnp.int32),
        "test_order": jax.random.permutation(streams_of[5], NTEST).astype(jnp.int32),
    }


def reference(train_feat, test_feat, kernel_inv, bucket_weight, bucket, test_order):
    acc = jnp.zeros((NTRAIN, NTEST), jnp.float32)
    for group_idx in range(N_CKPT):
        partial_sum = jnp.zeros((NTRAIN, NTEST), jnp.float32)
        for inner in range(CK_DEV):
            k = group_idx * CK_DEV + inner
            transformed = jnp.einsum("jb,ab->ja", test_feat[k], kernel_inv[k], preferred_element_type=jnp.float32).astype(jnp.bfloat16)
            ordered = jnp.zeros_like(transformed).at[test_order].set(transformed)
            weight = bucket_weight[k][bucket]
            partial_sum = partial_sum + weight[:, None] * jnp.dot(train_feat[k], ordered.T, preferred_element_type=jnp.float32)
        rounded = lax.optimization_barrier(partial_sum.astype(jnp.bfloat16))
        acc = acc + rounded.astype(jnp.float32)
    return acc / K
```

```python
import functools
import jax
import jax.numpy as jnp
from jax import lax
from jax.experimental import pallas as pl
from jax.experimental.pallas import tpu as pltpu
from jax.sharding import PartitionSpec as P

VMEM = pl.BlockSpec(memory_space=pltpu.VMEM)
SMEM = pl.BlockSpec(memory_space=pltpu.SMEM)
F32 = jnp.float32
LIMIT = 40 * 1024 * 1024


def factors(n):
    core = 2 if n % 2 == 0 else 1
    rest = n // core
    outer = 1
    while outer * outer < rest:
        outer *= 2
    if rest % outer:
        outer = rest
    return outer, rest // outer, core


def rotation(dims, axis, k):
    total = dims[0] * dims[1] * dims[2]
    pairs = []
    for dst in range(total):
        digits = [dst // (dims[1] * dims[2]), dst // dims[2] % dims[1], dst % dims[2]]
        digits[axis] = (digits[axis] + k) % dims[axis]
        pairs.append(((digits[0] * dims[1] + digits[1]) * dims[2] + digits[2], dst))
    return pairs


def gather(own, n):
    dims = factors(n)
    held = [((0, 0, 0), own)]
    for axis in range(3):
        arrived = []
        for k in range(1, dims[axis]):
            for offset, block in held:
                moved = list(offset)
                moved[axis] = k
                arrived.append(
                    (tuple(moved), lax.ppermute(block, "train", rotation(dims, axis, k)))
                )
        held = held + arrived
    me = lax.axis_index("train")
    mine = (me // (dims[1] * dims[2]), me // dims[2] % dims[1], me % dims[2])
    places = []
    for offset, _ in held:
        digit = [(mine[a] + offset[a]) % dims[a] for a in range(3)]
        places.append((digit[0] * dims[1] + digit[1]) * dims[2] + digit[2])
    return jnp.stack(places).astype(jnp.int32), [block for _, block in held]


def weights_kernel(bucket, table, out):
    rows = bucket.shape[1]
    onehot = (lax.broadcasted_iota(jnp.int32, (table.shape[0], rows), 0) == bucket[...]).astype(F32)
    out[...] = lax.dot_general(
        onehot, table[...], (((0,), (0,)), ((), ())),
        precision=lax.Precision.HIGHEST, preferred_element_type=F32,
    )


def transform_kernel(ensemble, places, me, order, *rest):
    blocks = rest[: -4]
    out, test, inverse, sorted_test = rest[-4:]
    rows = blocks[0].shape[1]
    for s, block in enumerate(blocks):
        at = pl.ds(pl.multiple_of(places[s] * rows, rows), rows)
        test[at, :] = block[0]
        inverse[at, :] = block[1]
    count = order.shape[1]
    width = count // ensemble
    for k in range(ensemble):
        first = lax.rem(me[0] + k, ensemble) * width
        wanted = lax.broadcasted_iota(jnp.int32, (width, count), 0) + first
        onehot = (wanted == order[...]).astype(jnp.bfloat16)
        sorted_test[...] = jnp.dot(
            onehot, test[...], preferred_element_type=F32
        ).astype(jnp.bfloat16)
        out[k] = lax.dot_general(
            inverse[...], sorted_test[...], (((1,), (1,)), ((), ())), preferred_element_type=F32
        ).astype(jnp.bfloat16)


def scaled(train, matrix, weight):
    tile = jnp.dot(train[...], matrix[...], preferred_element_type=F32)
    wide = jnp.concatenate([weight[...]] * (tile.shape[1] // weight.shape[1]), axis=1)
    return (tile * wide).astype(jnp.bfloat16)


def send_kernel(train, matrix, weight, out):
    out[...] = scaled(train, matrix, weight)


def sum_kernel(ensemble, train, matrix, weight, *rest):
    out = rest[-1]
    total = scaled(train, matrix, weight).astype(F32)
    for other in rest[:-2]:
        total = total + other[...].astype(F32)
    out[...] = total / ensemble


def shards(train_feat, test_feat, kernel_inv, bucket_weight, bucket, test_order):
    ensemble, n = lax.axis_size("ckpt"), lax.axis_size("train")
    train = train_feat[0]
    rows, size = train.shape
    count = test_order.shape[0]
    width = count // ensemble
    bf16 = jnp.bfloat16
    params = pltpu.CompilerParams(vmem_limit_bytes=LIMIT)

    places, blocks = gather(jnp.concatenate([test_feat, kernel_inv], axis=0), n)

    table = jnp.broadcast_to(bucket_weight.reshape(-1, 1), (bucket_weight.shape[1], 128))
    weight = pl.pallas_call(
        weights_kernel,
        out_shape=jax.ShapeDtypeStruct((rows, 128), F32),
        in_specs=[VMEM] * 2, out_specs=VMEM, compiler_params=params,
    )(bucket.reshape(1, rows), table)

    matrices = pl.pallas_call(
        functools.partial(transform_kernel, ensemble),
        out_shape=jax.ShapeDtypeStruct((ensemble, size, width), bf16),
        in_specs=[SMEM, SMEM, VMEM] + [VMEM] * len(blocks),
        out_specs=VMEM,
        scratch_shapes=[
            pltpu.VMEM((count, size), bf16),
            pltpu.VMEM((size, size), bf16),
            pltpu.VMEM((width, size), bf16),
        ],
        compiler_params=params,
        cost_estimate=pl.CostEstimate(
            flops=4 * size * size * count, bytes_accessed=8 * size * count, transcendentals=0
        ),
    )(places, lax.axis_index("ckpt").reshape(1), test_order.reshape(1, count), *blocks)

    parts = [1, 3, 3, 3, 3, 2, 1] if ensemble == 2 else [8, 8]
    unit = rows // sum(parts)
    starts = [sum(parts[:q]) * unit for q in range(len(parts))]

    def specs(first, length):
        step = unit
        at = first // step
        return (
            [
                pl.BlockSpec((step, size), lambda i: (at + i, 0)),
                None,
                pl.BlockSpec((step, 128), lambda i: (at + i, 0)),
            ],
            length // step,
            pl.BlockSpec((step, width), lambda i: (i, 0)),
            pl.BlockSpec((step, width), lambda i: (at + i, 0)),
        )

    received = []
    for first, part in zip(starts, parts):
        length = part * unit
        got = []
        for k in range(1, ensemble):
            ins, steps, moved, _ = specs(first, length)
            ins[1] = pl.BlockSpec((None, size, width), lambda i, k=k: (k, 0, 0))
            tile = pl.pallas_call(
                send_kernel,
                out_shape=jax.ShapeDtypeStruct((length, width), bf16),
                grid=(steps,), in_specs=ins, out_specs=moved, compiler_params=params,
                cost_estimate=pl.CostEstimate(
                    flops=2 * length * size * width,
                    bytes_accessed=2 * (length * size + size * width + length * width),
                    transcendentals=0,
                ),
            )(train, matrices, weight)
            got.append(
                lax.ppermute(tile, "ckpt", [(d, (d + k) % ensemble) for d in range(ensemble)])
            )
        received.append(got)

    out = jnp.zeros((rows, width), F32) if False else None
    for first, part, got in zip(starts, parts, received):
        length = part * unit
        ins, steps, moved, placed = specs(first, length)
        ins[1] = pl.BlockSpec((None, size, width), lambda i: (0, 0, 0))
        held = [] if out is None else [out]
        body = sum_kernel
        if out is None:
            def body(ensemble, *refs):
                sum_kernel(ensemble, *refs[:-1], None, refs[-1])
        out = pl.pallas_call(
            functools.partial(body, ensemble),
            out_shape=jax.ShapeDtypeStruct((rows, width), F32),
            grid=(steps,),
            in_specs=ins + [moved] * len(got) + [pl.BlockSpec(memory_space=pl.ANY)] * len(held),
            out_specs=placed,
            input_output_aliases={3 + len(got): 0} if held else {},
            compiler_params=params,
            cost_estimate=pl.CostEstimate(
                flops=2 * length * size * width,
                bytes_accessed=2 * (length * size + size * width + 3 * length * width),
                transcendentals=0,
            ),
        )(train, matrices, weight, *got, *held)
    return out


def solution(mesh):
    return jax.shard_map(
        shards,
        mesh=mesh,
        in_specs=(
            P("ckpt", "train", None),
            P("ckpt", "train", None),
            P("ckpt", "train", None),
            P("ckpt", None),
            P("train"),
            P(),
        ),
        out_specs=P("train", "ckpt"),
        check_vma=False,
    )
```

```python
import functools
import jax
import jax.numpy as jnp
from jax import lax
from jax.experimental import pallas as pl
from jax.experimental.pallas import tpu as pltpu
from jax.sharding import PartitionSpec as P

VMEM = pl.BlockSpec(memory_space=pltpu.VMEM)
SMEM = pl.BlockSpec(memory_space=pltpu.SMEM)
ANY = pl.BlockSpec(memory_space=pl.ANY)
F32 = jnp.float32
BF16 = jnp.bfloat16
MIB = 1024 * 1024
LANES = 128


def factors(n):
    core = 2 if n % 2 == 0 else 1
    rest = n // core
    outer = 1
    while outer * outer < rest:
        outer *= 2
    if rest % outer:
        outer = rest
    return outer, rest // outer, core


def turn(block, dims, axis, k):
    pairs = []
    for dst in range(dims[0] * dims[1] * dims[2]):
        digits = [dst // (dims[1] * dims[2]), dst // dims[2] % dims[1], dst % dims[2]]
        digits[axis] = (digits[axis] + k) % dims[axis]
        pairs.append(((digits[0] * dims[1] + digits[1]) * dims[2] + digits[2], dst))
    return lax.ppermute(block, "train", pairs)


def within(block, dims):
    held = [((0, 0), block)]
    held += [((k, 0), turn(block, dims, 1, k)) for k in range(1, dims[1])]
    held += [
        ((i, k), turn(b, dims, 2, k)) for k in range(1, dims[2]) for (i, _), b in held
    ]
    return [offset for offset, _ in held], [b for _, b in held]


def digits_of(me, dims):
    return (
        lax.div(me, dims[1] * dims[2]),
        lax.rem(lax.div(me, dims[2]), dims[1]),
        lax.rem(me, dims[2]),
    )


def inner_place(me, offset, dims):
    _, inner, core = digits_of(me, dims)
    return lax.rem(inner + offset[0], dims[1]) * dims[2] + lax.rem(core + offset[1], dims[2])


def outer_place(me, k, dims):
    return lax.rem(digits_of(me, dims)[0] + k, dims[0])


def ahead(k, n):
    return [(d, (d + k) % n) for d in range(n)]


def aligned(index, rows):
    return pl.ds(pl.multiple_of(index * rows, rows), rows)


def call(kernel, outs, operands, specs, mib=8, flops=0, moved=0, scratch=(), aliases=None, out_specs=None):
    several = isinstance(outs, list)
    shapes = outs if several else [outs]
    out_specs = out_specs or [VMEM] * len(shapes)
    return pl.pallas_call(
        kernel,
        out_shape=outs,
        in_specs=specs,
        out_specs=out_specs if several else out_specs[0],
        scratch_shapes=list(scratch),
        input_output_aliases=aliases or {},
        compiler_params=pltpu.CompilerParams(vmem_limit_bytes=mib * MIB),
        cost_estimate=pl.CostEstimate(flops=flops, bytes_accessed=moved, transcendentals=0),
    )(*operands)


def shape(dims, dtype=BF16):
    return jax.ShapeDtypeStruct(dims, dtype)


def stack_kernel(*refs):
    for i, ref in enumerate(refs[:-1]):
        refs[-1][i] = ref[...].reshape(refs[-1].shape[1:])


def weights_kernel(bucket, table, out):
    rows = bucket.shape[1]
    onehot = (lax.broadcasted_iota(jnp.int32, (table.shape[0], rows), 0) == bucket[...]).astype(F32)
    out[...] = lax.dot_general(
        onehot, table[...], (((0,), (0,)), ((), ())),
        precision=lax.Precision.HIGHEST, preferred_element_type=F32,
    )


def features_kernel(train, table, out, sem):
    rows = out.shape[0] - table.shape[0]
    copy = pltpu.make_async_copy(train.at[pl.ds(0, rows)], out.at[pl.ds(0, rows)], sem)
    copy.start()
    rest = table[...]
    for part in range(3):
        term = rest.astype(BF16)
        out[rows:, part * LANES : (part + 1) * LANES] = term
        rest = rest - term.astype(F32)
    out[rows:, 3 * LANES :] = jnp.zeros((table.shape[0], out.shape[1] - 3 * LANES), BF16)
    copy.wait()


def choose(ensemble, k, outer, me, order, test):
    width = order.shape[0] * order.shape[2] // ensemble
    first = lax.rem(me[0] + k, ensemble) * width
    wanted = lax.broadcasted_iota(jnp.int32, (width, order.shape[2]), 0) + first
    onehot = (wanted == order[outer]).astype(BF16)
    return jnp.dot(onehot, test[...], preferred_element_type=F32).astype(BF16)


def unpack(offsets, dims, me, k, blocks, test, inverse):
    rows = blocks[0].shape[1]
    outer = outer_place(me[1], k, dims)
    for offset, block in zip(offsets, blocks):
        at = inner_place(me[1], offset, dims)
        test[aligned(at, rows), :] = block[0]
        inverse[aligned(outer * len(blocks) + at, rows), :] = block[1]
    return outer


def part_kernel(ensemble, offsets, dims, k, me, order, *rest):
    blocks = rest[: len(offsets)]
    inverse, chosen, test = rest[-3:]
    outer = unpack(offsets, dims, me, k, blocks, test, inverse)
    width = chosen.shape[0] // ensemble
    for j in range(ensemble):
        rows = pl.ds(j * width, width)
        picked = choose(ensemble, j, outer, me, order, test)
        chosen[rows, :] = picked if k == 0 else chosen[rows, :] + picked


def transformed(inverse, chosen):
    return lax.dot_general(
        inverse[...], chosen, (((1,), (1,)), ((), ())), preferred_element_type=F32
    ).astype(BF16)


def send_transform_kernel(ensemble, offsets, dims, k, me, order, *rest):
    blocks = rest[: len(offsets)]
    inverse, chosen, test, out = rest[-4:]
    outer = unpack(offsets, dims, me, k, blocks, test, inverse)
    width = chosen.shape[0] // ensemble
    for j in range(1, ensemble):
        rows = pl.ds(j * width, width)
        picked = choose(ensemble, j, outer, me, order, test)
        if k > 0:
            picked = chosen[rows, :] + picked
        out[j - 1] = transformed(inverse, picked)


def own_transform_kernel(ensemble, dims, k, me, order, inverse, chosen, test, *rest):
    picked = choose(ensemble, 0, outer_place(me[1], k, dims), me, order, test)
    if k > 0:
        picked = chosen[: picked.shape[0], :] + picked
    rest[-1][...] = transformed(inverse, picked)


def scaled(train, matrix, weight):
    tile = jnp.dot(train, matrix, preferred_element_type=F32)
    wide = jnp.concatenate([weight] * (tile.shape[1] // weight.shape[1]), axis=1)
    return (tile * wide).astype(BF16)


def send_kernel(first, j, train, matrices, weight, *rest):
    out = rest[-1]
    rows = pl.ds(first, out.shape[0])
    out[...] = scaled(train[rows, :], matrices[j], weight[rows, :])


def first_kernel(first, me, train, matrices, weight, out, shard):
    send_kernel(first, 0, train, matrices, weight, out)
    shard[...] = matrices[0, aligned(me[1], shard.shape[0]), :]


def relay_kernel(block, *rest):
    rest[-1][...] = block[...]


def store(out, first, buffer, sems, step, tile):
    copies = []
    for i in range(buffer.shape[0] // step):
        at = i * step
        buffer[pl.ds(at, step), :] = tile(at)
        copies.append(
            pltpu.make_async_copy(
                buffer.at[pl.ds(at, step)], out.at[pl.ds(first + at, step)], sems.at[i]
            )
        )
        copies[-1].start()
    for copy in copies:
        copy.wait()


def sum_kernel(ensemble, others, first, step, train, matrix, weight, *rest):
    got = rest[:others]
    out, token, buffer, sems = rest[-4:]
    token[...] = jnp.zeros_like(token)

    def tile(at):
        rows = pl.ds(first + at, step)
        total = scaled(train[rows, :], matrix[...], weight[rows, :]).astype(F32)
        for other in got:
            total = total + other[pl.ds(at, step), :].astype(F32)
        return total / ensemble

    store(out, first, buffer, sems, step, tile)


def both_kernel(ensemble, dims, offsets, step, me, train, matrix, weight, bucket, train2, *rest):
    pieces = rest[: len(offsets)]
    out, token, matrix2, weight2, buffer, sems = rest[-6:]
    token[...] = jnp.zeros_like(token)
    count = buffer.shape[0]
    table = jnp.zeros((train2.shape[0] - count, LANES), F32)
    for part in range(3):
        table = table + train2[count:, part * LANES : (part + 1) * LANES].astype(F32)
    onehot = (
        lax.broadcasted_iota(jnp.int32, (table.shape[0], count), 0) == bucket[:, :count]
    ).astype(F32)
    weight2[...] = lax.dot_general(
        onehot, table, (((0,), (0,)), ((), ())),
        precision=lax.Precision.HIGHEST, preferred_element_type=F32,
    )
    rows = pieces[0].shape[1]
    for offset, piece in zip(offsets, pieces):
        at = inner_place(me[1], offset, dims)
        for k in range(dims[0]):
            index = outer_place(me[1], k, dims) * len(offsets) + at
            matrix2[aligned(index, rows), :] = piece[k]

    def tile(at):
        rows = pl.ds(at, step)
        total = scaled(train[rows, :], matrix[...], weight[rows, :]).astype(F32)
        total = total + scaled(train2[rows, :], matrix2[...], weight2[rows, :]).astype(F32)
        return total / ensemble

    store(out, 0, buffer, sems, step, tile)


def shards(train_feat, test_feat, kernel_inv, bucket_weight, bucket, test_order):
    ensemble, n = lax.axis_size("ckpt"), lax.axis_size("train")
    dims = factors(n)
    train = train_feat[0]
    rows, size = train.shape
    count = test_order.shape[0]
    width = count // ensemble
    unit = rows // 16
    paired = ensemble == 2
    featured = 6 if paired else 0
    parts = [1, 2, 2, 2, 2, 1] if paired else [8, 8]
    buckets = bucket_weight.shape[1]
    table_rows = -(-buckets // 16) * 16

    me = jnp.stack([lax.axis_index("ckpt"), lax.axis_index("train")]).astype(jnp.int32)
    order = test_order.reshape(dims[0], 1, count // dims[0])
    bucket = bucket.reshape(1, rows)
    table = jnp.broadcast_to(bucket_weight.reshape(buckets, 1), (buckets, LANES))
    table = jnp.pad(table, ((0, table_rows - buckets), (0, 0)))

    own = call(
        stack_kernel, shape((2, test_feat.shape[1], size)), (test_feat, kernel_inv), [VMEM] * 2
    )
    early = []
    if paired:
        features = call(
            features_kernel, shape((featured * unit + table_rows, size)), (train, table),
            [ANY, VMEM], scratch=[pltpu.SemaphoreType.DMA],
        )
        train2 = lax.ppermute(features, "ckpt", ahead(1, ensemble))
        early = [train2]

    outer = [own] + [turn(own, dims, 0, k) for k in range(1, dims[0])]
    groups = [within(block, dims) for block in outer]
    weight = call(weights_kernel, shape((rows, LANES), F32), (bucket, table), [VMEM] * 2)

    half = 2 * size * size * width
    state, last = [], dims[0] - 1
    for k, (offsets, blocks) in enumerate(groups[:-1]):
        operands = [me, order, *blocks, *state]
        state = call(
            functools.partial(part_kernel, ensemble, offsets, dims, k),
            [shape((size, size)), shape((count, size))],
            operands, [SMEM] + [VMEM] * (len(operands) - 1),
            scratch=[pltpu.VMEM((count // dims[0], size), BF16)],
            aliases={len(operands) - 2: 0, len(operands) - 1: 1} if state else None,
            flops=4 * half, moved=4 * size * size,
        )
    offsets, blocks = groups[-1]
    operands = [me, order, *blocks, *state, *early]
    aliases = {2 + len(blocks): 0, 3 + len(blocks): 1} if state else None
    inverse, chosen, test, matrices = call(
        functools.partial(send_transform_kernel, ensemble, offsets, dims, last),
        [
            shape((size, size)), shape((count, size)), shape((count // dims[0], size)),
            shape((ensemble - 1, size, width)),
        ],
        operands, [SMEM] + [VMEM] * (1 + len(blocks) + len(state)) + [ANY] * len(early),
        aliases=aliases, flops=3 * half, moved=4 * size * size, mib=12,
    )

    def send(first, part, after):
        got = []
        for k in range(1, ensemble):
            tile = call(
                functools.partial(send_kernel, first * unit, k - 1),
                shape((part * unit, width)),
                (train, matrices, weight, *after), [VMEM] * 3 + [ANY] * len(after),
                flops=2 * part * unit * size * width, moved=2 * part * unit * (size + width),
            )
            after = [tile]
            got.append(lax.ppermute(tile, "ckpt", ahead(k, ensemble)))
        return got, after

    starts = [featured + sum(parts[:q]) for q in range(len(parts))]
    flying = 3
    received, after = [], []
    for q in range(min(flying, len(parts))):
        if q == 0 and paired:
            tile, shard = call(
                functools.partial(first_kernel, starts[0] * unit),
                [shape((parts[0] * unit, width)), shape((size // n, width))],
                (me, train, matrices, weight), [SMEM] + [VMEM] * 3,
                flops=2 * parts[0] * unit * size * width, moved=2 * parts[0] * unit * (size + width),
            )
            got, after = [lax.ppermute(tile, "ckpt", ahead(1, ensemble))], [tile]
        else:
            got, after = send(starts[q], parts[q], after)
        received.append(got)
        if q == 1 and paired:
            shard2 = lax.ppermute(shard, "ckpt", ahead(1, ensemble))
            shard2 = call(relay_kernel, shape(shard2.shape), (shard2, *after), [VMEM] + [ANY] * len(after))
            column = call(
                stack_kernel, shape((dims[0],) + shard.shape),
                [shard2] + [turn(shard2, dims, 0, k) for k in range(1, dims[0])],
                [VMEM] * dims[0],
            )
            piece_offsets, pieces = within(column, dims)
        if q == min(1, len(parts) - 1):
            matrix = call(
                functools.partial(own_transform_kernel, ensemble, dims, last),
                shape((size, width)), (me, order, inverse, chosen, test, *after),
                [SMEM] + [VMEM] * 4 + [ANY] * len(after), flops=3 * half, moved=4 * size * size, mib=12,
            )
            after = [matrix]

    out = None

    def put(kernel, first, part, step, operands, specs, scratch=()):
        held = [] if out is None else [out]
        return call(
            kernel, [shape((rows, width), F32), shape((8, LANES), F32)],
            (*operands, *held), specs + [ANY] * len(held),
            out_specs=[ANY, VMEM],
            scratch=[
                *scratch, pltpu.VMEM((part * unit, width), F32),
                pltpu.SemaphoreType.DMA((part * unit // step,)),
            ],
            aliases={len(operands): 0} if held else None, mib=16,
            flops=2 * part * unit * size * width, moved=2 * part * unit * (size + 3 * width),
        )

    for q, (first, part) in enumerate(zip(starts, parts)):
        if paired and q == max(len(parts) - 2, 0):
            out, token = put(
                functools.partial(both_kernel, ensemble, dims, piece_offsets, unit),
                0, featured, unit,
                (me, train, matrix, weight, bucket, train2, *pieces),
                [SMEM] + [VMEM] * (5 + len(pieces)),
                scratch=[
                    pltpu.VMEM((size, width), BF16), pltpu.VMEM((featured * unit, LANES), F32)
                ],
            )
        got = received[q]
        out, token = put(
            functools.partial(sum_kernel, ensemble, len(got), first * unit, unit),
            first, part, unit, (train, matrix, weight, *got), [VMEM] * (3 + len(got)),
        )
        if q + flying < len(parts):
            more, _ = send(starts[q + flying], parts[q + flying], [token])
            received.append(more)
    return out


def solution(mesh):
    return jax.shard_map(
        shards,
        mesh=mesh,
        in_specs=(
            P("ckpt", "train", None),
            P("ckpt", "train", None),
            P("ckpt", "train", None),
            P("ckpt", None),
            P("train"),
            P(),
        ),
        out_specs=P("train", "ckpt"),
        check_vma=False,
    )
```

```python
import functools
import jax
import jax.numpy as jnp
from jax import lax
from jax.experimental import pallas as pl
from jax.experimental.pallas import tpu as pltpu
from jax.sharding import PartitionSpec as P

VMEM = pl.BlockSpec(memory_space=pltpu.VMEM)
SMEM = pl.BlockSpec(memory_space=pltpu.SMEM)
ANY = pl.BlockSpec(memory_space=pl.ANY)
F32 = jnp.float32
BF16 = jnp.bfloat16
MIB = 1024 * 1024
LANES = 128


def bits_of(n):
    bits = [1 << i for i in reversed(range(n.bit_length() - 1))]
    assert n == 1 << len(bits)
    core = bits[-1:]
    rest = bits[:-1]
    cut = (len(rest) + 1) // 2
    return rest[:cut], rest[cut:], core


def swap(block, mask, n):
    return lax.ppermute(block, "train", [(d ^ mask, d) for d in range(n)])


def spread(block, bits, n, start=0):
    return spread_on([(start, block)], bits, n)


def spread_on(held, bits, n):
    for bit in bits:
        held += [(mask ^ bit, swap(b, bit, n)) for mask, b in held]
    return sorted(held, key=lambda entry: entry[0])


def masks_of(bits):
    masks = [0]
    for bit in bits:
        masks += [mask ^ bit for mask in masks]
    return sorted(masks)


def ahead(k, n):
    return [(d, (d + k) % n) for d in range(n)]


def aligned(index, rows):
    return pl.ds(pl.multiple_of(index * rows, rows), rows)


def call(kernel, outs, operands, specs, mib=8, flops=0, moved=0, scratch=(), aliases=None, out_specs=None):
    several = isinstance(outs, list)
    out_specs = out_specs or [VMEM] * (len(outs) if several else 1)
    return pl.pallas_call(
        kernel,
        out_shape=outs,
        in_specs=specs,
        out_specs=out_specs if several else out_specs[0],
        scratch_shapes=list(scratch),
        input_output_aliases=aliases or {},
        compiler_params=pltpu.CompilerParams(vmem_limit_bytes=mib * MIB),
        cost_estimate=pl.CostEstimate(flops=flops, bytes_accessed=moved, transcendentals=0),
    )(*operands)


def shape(dims, dtype=BF16):
    return jax.ShapeDtypeStruct(dims, dtype)


def table_of(bucket_weight, rows):
    count = bucket_weight.shape[1]
    at = lax.broadcasted_iota(jnp.int32, (rows, count), 0)
    lane = lax.broadcasted_iota(jnp.int32, (rows, count), 1)
    column = jnp.sum(jnp.where(at == lane, bucket_weight, 0.0), axis=1, keepdims=True)
    return jnp.broadcast_to(column, (rows, LANES))


def weights_of(bucket, table):
    onehot = lax.broadcasted_iota(jnp.int32, (table.shape[0], bucket.shape[1]), 0) == bucket
    return lax.dot_general(
        onehot.astype(F32), table, (((0,), (0,)), ((), ())),
        precision=lax.Precision.HIGHEST, preferred_element_type=F32,
    )


def weights_kernel(table_rows, bucket, bucket_weight, out):
    out[...] = weights_of(bucket[...], table_of(bucket_weight[...], table_rows))


def start_kernel(steps, test_feat, kernel_inv, train, bucket_weight, own, *rest):
    batches, (pair, held, below, sems) = rest[:-4], rest[-4:]
    moves = [(test_feat.at[0], pair.at[0], own.at[0]), (kernel_inv.at[0], pair.at[1], own.at[1])]
    count = below.shape[0]
    first = 0
    for i, batch in enumerate(batches):
        step = (batch.shape[0] - (0 if i else count)) // steps
        for i in range(steps):
            span = pl.ds(first + i * step, step)
            moves.append((train.at[span], held.at[span], batch.at[pl.ds(i * step, step)]))
        first += steps * step
    ins = [
        pltpu.make_async_copy(source, middle, sems.at[0, i])
        for i, (source, middle, _) in enumerate(moves)
    ]
    outs = [
        pltpu.make_async_copy(middle, target, sems.at[1, i])
        for i, (_, middle, target) in enumerate(moves)
    ]
    for copy in ins:
        copy.start()
    if batches:
        left = table_of(bucket_weight[...], count)
        for part in range(3):
            term = left.astype(BF16)
            below[:, part * LANES : (part + 1) * LANES] = term
            left = left - term.astype(F32)
        below[:, 3 * LANES :] = jnp.zeros((count, below.shape[1] - 3 * LANES), BF16)
        span = pl.ds(batches[0].shape[0] - count, count)
        outs.append(pltpu.make_async_copy(below, batches[0].at[span], sems.at[1, len(moves)]))
        outs[-1].start()
    for inward, outward in zip(ins, outs):
        inward.wait()
        outward.start()
    for copy in outs:
        copy.wait()


def choose(ensemble, k, outer, ckpt, order, test):
    width = order.shape[0] * order.shape[2] // ensemble
    first = lax.rem(ckpt[0] + k, ensemble) * width
    wanted = lax.broadcasted_iota(jnp.int32, (width, order.shape[2]), 0) + first
    onehot = (wanted == order[outer]).astype(BF16)
    return jnp.dot(onehot, test[...], preferred_element_type=F32).astype(BF16)


def unpack(masks, me, blocks, test, inverse):
    rows = blocks[0].shape[1]
    for mask, block in zip(masks, blocks):
        at = lax.bitwise_xor(me[0], mask)
        test[aligned(lax.rem(at, len(masks)), rows), :] = block[0]
        inverse[aligned(at, rows), :] = block[1]
    return lax.div(lax.bitwise_xor(me[0], masks[0]), len(masks))


def part_kernel(ensemble, masks, ckpt, me, order, *rest):
    blocks = rest[: len(masks)]
    inverse, chosen, test = rest[-3:]
    outer = unpack(masks, me, blocks, test, inverse)
    width = chosen.shape[0] // ensemble
    for j in range(ensemble):
        rows = pl.ds(j * width, width)
        picked = choose(ensemble, j, outer, ckpt, order, test)
        chosen[rows, :] = picked if masks[0] == 0 else chosen[rows, :] + picked


def transformed(inverse, chosen):
    return lax.dot_general(
        inverse[...], chosen, (((1,), (1,)), ((), ())), preferred_element_type=F32
    ).astype(BF16)


def send_transform_kernel(ensemble, masks, ckpt, me, order, *rest):
    blocks = rest[: len(masks)]
    inverse, chosen, test, out = rest[-4:]
    outer = unpack(masks, me, blocks, test, inverse)
    width = chosen.shape[0] // ensemble
    for j in range(1, ensemble):
        picked = choose(ensemble, j, outer, ckpt, order, test)
        out[j - 1] = transformed(inverse, chosen[pl.ds(j * width, width), :] + picked)


def own_transform_kernel(ensemble, masks, ckpt, me, order, inverse, chosen, test, *rest):
    outer = lax.div(lax.bitwise_xor(me[0], masks[0]), len(masks))
    picked = choose(ensemble, 0, outer, ckpt, order, test)
    rest[-1][...] = transformed(inverse, chosen[: picked.shape[0], :] + picked)


def scaled(train, matrix, weight):
    tile = jnp.dot(train, matrix, preferred_element_type=F32)
    wide = jnp.concatenate([weight] * (tile.shape[1] // weight.shape[1]), axis=1)
    return (tile * wide).astype(BF16)


def send_kernel(first, length, j, train, matrices, weight, *rest):
    rows = pl.ds(first, length)
    rest[-1][:length, :] = scaled(train[rows, :], matrices[j], weight[rows, :])


def first_kernel(first, length, me, train, matrices, weight, out):
    send_kernel(first, length, 0, train, matrices, weight, out)
    out[length:, :] = matrices[0, aligned(me[0], out.shape[0] - length), :]


def tail_kernel(first, block, *rest):
    rest[-1][...] = block[first:, :]


def relay_kernel(block, *rest):
    rest[-1][...] = block[...]


def stack_kernel(count, *refs):
    for i, ref in enumerate(refs[:count]):
        refs[-1][i] = ref[...]


def store(out, first, at, buffer, sems, tile):
    rows = tile.shape[0] // len(sems)
    copies = []
    for i, sem in enumerate(sems):
        span = pl.ds(at + i * rows, rows)
        buffer[span, :] = tile[i * rows : (i + 1) * rows]
        copies.append(
            pltpu.make_async_copy(buffer.at[span], out.at[pl.ds(first + at + i * rows, rows)], sem)
        )
        copies[-1].start()
    return copies


def sums(ensemble, first, at, train, matrix, weight, got, out, buffer, sems, length):
    rows = pl.ds(first, length)
    total = scaled(train[rows, :], matrix[...], weight[rows, :]).astype(F32)
    for other in got:
        total = total + other[:length, :].astype(F32)
    return store(out, first - at, at, buffer, sems, total / ensemble)


def sum_kernel(ensemble, first, lengths, train, matrix, weight, *rest):
    out, buffer, sems = rest[-3:]
    copies, at, others = [], 0, ensemble - 1
    for i, length in enumerate(lengths):
        got = rest[i * others : (i + 1) * others]
        two = [sems.at[2 * i], sems.at[2 * i + 1]]
        copies += sums(
            ensemble, first + at, at, train, matrix, weight, got, out, buffer, two, length
        )
        at += length
    for copy in copies:
        copy.wait()


def both_kernel(ensemble, masks, outers, batches, me, train, matrix, weight, bucket, *rest):
    features, pieces = rest[:batches], rest[batches : batches + len(masks)]
    out, matrix2, weight2, buffer, sems = rest[-5:]
    count = buffer.shape[0]
    extra = sum(batch.shape[0] for batch in features) - count
    table = jnp.zeros((extra, LANES), F32)
    for part in range(3):
        lanes = pl.ds(part * LANES, LANES)
        table = table + features[0][features[0].shape[0] - extra :, lanes].astype(F32)
    weight2[...] = weights_of(bucket[:, :count], table)
    rows = pieces[0].shape[1]
    for mask, piece in zip(masks, pieces):
        for i, outer in enumerate(outers):
            at = lax.bitwise_xor(me[0], mask ^ outer)
            matrix2[aligned(at, rows), :] = piece[i]
    copies, first = [], 0
    for i, batch in enumerate(features):
        each = batch.shape[0] - (0 if i else extra)
        rows = pl.ds(first, each)
        total = scaled(train[rows, :], matrix[...], weight[rows, :]).astype(F32)
        total = total + scaled(batch[:each, :], matrix2[...], weight2[rows, :]).astype(F32)
        two = [sems.at[2 * i], sems.at[2 * i + 1]]
        copies += store(out, 0, first, buffer, two, total / ensemble)
        first += each
    for copy in copies:
        copy.wait()


def shards(train_feat, test_feat, kernel_inv, bucket_weight, bucket, test_order):
    ensemble, n = lax.axis_size("ckpt"), lax.axis_size("train")
    outer_bits, inner_bits, core_bits = bits_of(n)
    outers = masks_of(outer_bits)
    inners = masks_of(inner_bits + core_bits)
    train = train_feat[0]
    rows, size = train.shape
    count = test_order.shape[0]
    width = count // ensemble
    share = size // n
    unit = rows // 32
    paired = ensemble == 2
    batches = [6, 6] if paired else []
    featured = sum(batches)
    parts = [1, 10, 5, 4] if paired else [16, 16]
    flying = 2
    table_rows = -(-bucket_weight.shape[1] // 16) * 16

    ckpt = lax.axis_index("ckpt").astype(jnp.int32).reshape(1)
    me = lax.axis_index("train").astype(jnp.int32).reshape(1)
    order = test_order.reshape(len(outers), 1, count // len(outers))
    bucket = bucket.reshape(1, rows)

    sent = [shape((part * unit + (0 if i else table_rows), size)) for i, part in enumerate(batches)]
    steps = 2
    own, *features = call(
        functools.partial(start_kernel, steps),
        [shape((2, test_feat.shape[1], size)), *sent],
        (test_feat, kernel_inv, train, bucket_weight), [ANY] * 3 + [VMEM],
        out_specs=[ANY] * (1 + len(sent)), mib=60,
        scratch=[
            pltpu.VMEM((2, test_feat.shape[1], size), BF16),
            pltpu.VMEM((max(featured, 1) * unit, size), BF16),
            pltpu.VMEM((table_rows, size), BF16),
            pltpu.SemaphoreType.DMA((2, 3 + steps * len(sent))),
        ],
    )
    features = [lax.ppermute(batch, "ckpt", ahead(1, ensemble)) for batch in features]

    groups = []
    for mask, block in sorted(spread(own, outer_bits, n), key=lambda e: e[0]):
        held = [(mask, block)]
        inner = spread(block, inner_bits, n, mask)[1:]
        held = spread_on(held + inner, core_bits, n)
        groups.append(([m for m, _ in held], [b for _, b in held]))
    weight = call(
        functools.partial(weights_kernel, table_rows), shape((rows, LANES), F32),
        (bucket, bucket_weight), [VMEM] * 2,
    )

    half = 2 * size * size * width
    state = []
    for masks, blocks in groups[:-1]:
        operands = [ckpt, me, order, *blocks, *state]
        after = features[:1] if not state else []
        state = call(
            functools.partial(part_kernel, ensemble, masks),
            [shape((size, size)), shape((count, size))],
            [*operands, *after], [SMEM] * 2 + [VMEM] * (len(operands) - 2) + [ANY] * len(after),
            scratch=[pltpu.VMEM((count // len(outers), size), BF16)],
            aliases={len(operands) - 2: 0, len(operands) - 1: 1} if state else None,
            flops=4 * half, moved=4 * size * size,
        )
    masks, blocks = groups[-1]
    inverse, chosen, test, matrices = call(
        functools.partial(send_transform_kernel, ensemble, masks),
        [
            shape((size, size)), shape((count, size)), shape((count // len(outers), size)),
            shape((ensemble - 1, size, width)),
        ],
        [ckpt, me, order, *blocks, *state],
        [SMEM] * 2 + [VMEM] * (3 + len(blocks)),
        aliases={3 + len(blocks): 0, 4 + len(blocks): 1},
        flops=3 * half, moved=4 * size * size, mib=12,
    )

    def send(first, part, after):
        got = []
        for k in range(1, ensemble):
            tile = call(
                functools.partial(send_kernel, first * unit, part * unit, k - 1),
                shape((part * unit, width)),
                (train, matrices, weight, *after), [VMEM] * 3 + [ANY] * len(after),
            )
            after = [tile]
            got.append(lax.ppermute(tile, "ckpt", ahead(k, ensemble)))
        return got, after

    starts = [featured + sum(parts[:q]) for q in range(len(parts))]
    received, after = [], []
    if paired:
        tile = call(
            functools.partial(first_kernel, starts[0] * unit, parts[0] * unit),
            shape((parts[0] * unit + share, width)),
            (me, train, matrices, weight), [SMEM] + [VMEM] * 3,
        )
        received.append([lax.ppermute(tile, "ckpt", ahead(1, ensemble))])
        after = [tile]
    for q in range(len(received), min(flying, len(parts))):
        got, after = send(starts[q], parts[q], after)
        received.append(got)
    if paired:
        piece = call(
            functools.partial(tail_kernel, parts[0] * unit), shape((share, width)),
            (*received[0], *after), [VMEM, ANY],
        )
        after = [piece]

    matrix = call(
        functools.partial(own_transform_kernel, ensemble, masks),
        shape((size, width)), (ckpt, me, order, inverse, chosen, test, *after, *features[1:]),
        [SMEM] * 2 + [VMEM] * 4 + [ANY] * (len(after) + len(features[1:])), flops=3 * half, mib=12,
    )
    if paired:
        got, after = send(starts[flying], parts[flying], after)
        received.append(got)
        column = call(
            functools.partial(stack_kernel, len(outers)), shape((len(outers), share, width)),
            [piece] + [swap(piece, mask, n) for mask in outers[1:]] + [matrix],
            [VMEM] * len(outers) + [ANY],
        )
        for q in range(flying + 1, len(parts)):
            got, after = send(starts[q], parts[q], [column])
            received.append(got)
        held = [(0, column)]
        for bit in inner_bits:
            held += [(mask ^ bit, swap(b, bit, n)) for mask, b in held]
        held = held[:1] + [
            (mask, call(relay_kernel, shape(b.shape), (b, *received[1]), [VMEM, ANY]))
            for mask, b in held[1:]
        ]
        for bit in core_bits:
            held += [(mask ^ bit, swap(b, bit, n)) for mask, b in held]
        pieces = [b for _, b in sorted(held, key=lambda entry: entry[0])]

    out = None

    def put(kernel, part, copies, operands, specs, scratch=()):
        held = [] if out is None else [out]
        return call(
            kernel, shape((rows, width), F32),
            (*operands, *held), specs + [ANY] * len(held),
            out_specs=[ANY],
            scratch=[
                *scratch, pltpu.VMEM((part * unit, width), F32), pltpu.SemaphoreType.DMA((copies,)),
            ],
            aliases={len(operands): 0} if held else None, mib=24,
        )

    together = [[0, 1], [], [2, 3]] if paired else [[q] for q in range(len(parts))]
    for chunks in together:
        if chunks:
            part = sum(parts[q] for q in chunks)
            got = [tile for q in chunks for tile in received[q]]
            lengths = [parts[q] * unit for q in chunks]
            out = put(
                functools.partial(sum_kernel, ensemble, starts[chunks[0]] * unit, lengths),
                part, 2 * len(chunks), (train, matrix, weight, *got), [VMEM] * (3 + len(got)),
            )
        else:
            out = put(
                functools.partial(both_kernel, ensemble, inners, outers, len(batches)),
                featured, 2 * len(batches),
                (me, train, matrix, weight, bucket, *features, *pieces),
                [SMEM] + [VMEM] * (4 + len(features) + len(pieces)),
                scratch=[
                    pltpu.VMEM((size, width), BF16), pltpu.VMEM((featured * unit, LANES), F32)
                ],
            )
    return out


def solution(mesh):
    return jax.shard_map(
        shards,
        mesh=mesh,
        in_specs=(
            P("ckpt", "train", None),
            P("ckpt", "train", None),
            P("ckpt", "train", None),
            P("ckpt", None),
            P("train"),
            P(),
        ),
        out_specs=P("train", "ckpt"),
        check_vma=False,
    )
```

```python
import functools
import jax
import jax.numpy as jnp
from jax import lax
from jax.experimental import pallas as pl
from jax.experimental.pallas import tpu as pltpu
from jax.sharding import PartitionSpec as P

VMEM = pl.BlockSpec(memory_space=pltpu.VMEM)
SMEM = pl.BlockSpec(memory_space=pltpu.SMEM)
ANY = pl.BlockSpec(memory_space=pl.ANY)
F32 = jnp.float32
BF16 = jnp.bfloat16
MIB = 1024 * 1024
LANES = 128


def bits_of(n):
    bits = [1 << i for i in reversed(range(n.bit_length() - 1))]
    assert n == 1 << len(bits)
    core = bits[-1:]
    rest = bits[:-1]
    cut = (len(rest) + 1) // 2
    return rest[:cut], rest[cut:], core


def swap(block, mask, n):
    return lax.ppermute(block, "train", [(d ^ mask, d) for d in range(n)])


def spread(block, bits, n, start=0):
    return spread_on([(start, block)], bits, n)


def spread_on(held, bits, n):
    for bit in bits:
        held += [(mask ^ bit, swap(b, bit, n)) for mask, b in held]
    return sorted(held, key=lambda entry: entry[0])


def masks_of(bits):
    masks = [0]
    for bit in bits:
        masks += [mask ^ bit for mask in masks]
    return sorted(masks)


def ahead(k, n):
    return [(d, (d + k) % n) for d in range(n)]


def aligned(index, rows):
    return pl.ds(pl.multiple_of(index * rows, rows), rows)


def call(kernel, outs, operands, specs, mib=8, flops=0, moved=0, scratch=(), aliases=None, out_specs=None):
    several = isinstance(outs, list)
    out_specs = out_specs or [VMEM] * (len(outs) if several else 1)
    return pl.pallas_call(
        kernel,
        out_shape=outs,
        in_specs=specs,
        out_specs=out_specs if several else out_specs[0],
        scratch_shapes=list(scratch),
        input_output_aliases=aliases or {},
        compiler_params=pltpu.CompilerParams(vmem_limit_bytes=mib * MIB),
        cost_estimate=pl.CostEstimate(flops=flops, bytes_accessed=moved, transcendentals=0),
    )(*operands)


def shape(dims, dtype=BF16):
    return jax.ShapeDtypeStruct(dims, dtype)


def table_of(bucket_weight, rows):
    count = bucket_weight.shape[1]
    at = lax.broadcasted_iota(jnp.int32, (rows, count), 0)
    lane = lax.broadcasted_iota(jnp.int32, (rows, count), 1)
    column = jnp.sum(jnp.where(at == lane, bucket_weight, 0.0), axis=1, keepdims=True)
    return jnp.broadcast_to(column, (rows, LANES))


def weights_of(bucket, table):
    onehot = lax.broadcasted_iota(jnp.int32, (table.shape[0], bucket.shape[1]), 0) == bucket
    return lax.dot_general(
        onehot.astype(F32), table, (((0,), (0,)), ((), ())),
        precision=lax.Precision.HIGHEST, preferred_element_type=F32,
    )


def weights_kernel(table_rows, bucket, bucket_weight, out):
    out[...] = weights_of(bucket[...], table_of(bucket_weight[...], table_rows))


def start_kernel(steps, test_feat, kernel_inv, train, bucket_weight, own, *rest):
    batches, (pair, held, below, sems) = rest[:-4], rest[-4:]
    moves = [(test_feat.at[0], pair.at[0], own.at[0]), (kernel_inv.at[0], pair.at[1], own.at[1])]
    count = below.shape[0]
    first = 0
    for i, batch in enumerate(batches):
        step = (batch.shape[0] - (0 if i else count)) // steps
        for i in range(steps):
            span = pl.ds(first + i * step, step)
            moves.append((train.at[span], held.at[span], batch.at[pl.ds(i * step, step)]))
        first += steps * step
    ins = [
        pltpu.make_async_copy(source, middle, sems.at[0, i])
        for i, (source, middle, _) in enumerate(moves)
    ]
    outs = [
        pltpu.make_async_copy(middle, target, sems.at[1, i])
        for i, (_, middle, target) in enumerate(moves)
    ]
    for copy in ins:
        copy.start()
    if batches:
        left = table_of(bucket_weight[...], count)
        for part in range(3):
            term = left.astype(BF16)
            below[:, part * LANES : (part + 1) * LANES] = term
            left = left - term.astype(F32)
        below[:, 3 * LANES :] = jnp.zeros((count, below.shape[1] - 3 * LANES), BF16)
        span = pl.ds(batches[0].shape[0] - count, count)
        outs.append(pltpu.make_async_copy(below, batches[0].at[span], sems.at[1, len(moves)]))
        outs[-1].start()
    for inward, outward in zip(ins, outs):
        inward.wait()
        outward.start()
    for copy in outs:
        copy.wait()


def choose(ensemble, k, outer, ckpt, order, test):
    width = order.shape[0] * order.shape[2] // ensemble
    first = lax.rem(ckpt[0] + k, ensemble) * width
    wanted = lax.broadcasted_iota(jnp.int32, (width, order.shape[2]), 0) + first
    onehot = (wanted == order[outer]).astype(BF16)
    return jnp.dot(onehot, test[...], preferred_element_type=F32).astype(BF16)


def unpack(masks, me, blocks, test, inverse):
    rows = blocks[0].shape[1]
    for mask, block in zip(masks, blocks):
        at = lax.bitwise_xor(me[0], mask)
        test[aligned(lax.rem(at, len(masks)), rows), :] = block[0]
        inverse[aligned(at, rows), :] = block[1]
    return lax.div(lax.bitwise_xor(me[0], masks[0]), len(masks))


def part_kernel(ensemble, masks, ckpt, me, order, *rest):
    blocks = rest[: len(masks)]
    inverse, chosen, test = rest[-3:]
    outer = unpack(masks, me, blocks, test, inverse)
    width = chosen.shape[0] // ensemble
    for j in range(ensemble):
        rows = pl.ds(j * width, width)
        picked = choose(ensemble, j, outer, ckpt, order, test)
        chosen[rows, :] = picked if masks[0] == 0 else chosen[rows, :] + picked


def transformed(inverse, chosen):
    return lax.dot_general(
        inverse[...], chosen, (((1,), (1,)), ((), ())), preferred_element_type=F32
    ).astype(BF16)


def send_transform_kernel(ensemble, masks, ckpt, me, order, *rest):
    blocks = rest[: len(masks)]
    inverse, chosen, test, out = rest[-4:]
    outer = unpack(masks, me, blocks, test, inverse)
    width = chosen.shape[0] // ensemble
    for j in range(1, ensemble):
        picked = choose(ensemble, j, outer, ckpt, order, test)
        out[j - 1] = transformed(inverse, chosen[pl.ds(j * width, width), :] + picked)


def own_transform_kernel(ensemble, masks, ckpt, me, order, inverse, chosen, test, *rest):
    outer = lax.div(lax.bitwise_xor(me[0], masks[0]), len(masks))
    picked = choose(ensemble, 0, outer, ckpt, order, test)
    rest[-1][...] = transformed(inverse, chosen[: picked.shape[0], :] + picked)


def scaled(train, matrix, weight):
    tile = jnp.dot(train, matrix, preferred_element_type=F32)
    wide = jnp.concatenate([weight] * (tile.shape[1] // weight.shape[1]), axis=1)
    return (tile * wide).astype(BF16)


def send_kernel(first, length, j, train, matrices, weight, *rest):
    rows = pl.ds(first, length)
    rest[-1][:length, :] = scaled(train[rows, :], matrices[j], weight[rows, :])


def first_kernel(first, length, me, train, matrices, weight, out):
    send_kernel(first, length, 0, train, matrices, weight, out)
    out[length:, :] = matrices[0, aligned(me[0], out.shape[0] - length), :]


def tail_kernel(first, block, *rest):
    rest[-1][...] = block[first:, :]


def relay_kernel(block, *rest):
    rest[-1][...] = block[...]


def stack_kernel(count, *refs):
    for i, ref in enumerate(refs[:count]):
        refs[-1][i] = ref[...]


def store(out, first, at, buffer, sems, tile):
    rows = tile.shape[0] // len(sems)
    copies = []
    for i, sem in enumerate(sems):
        span = pl.ds(at + i * rows, rows)
        buffer[span, :] = tile[i * rows : (i + 1) * rows]
        copies.append(
            pltpu.make_async_copy(buffer.at[span], out.at[pl.ds(first + at + i * rows, rows)], sem)
        )
        copies[-1].start()
    return copies


def sums(ensemble, first, at, train, matrix, weight, got, out, buffer, sems, length):
    rows = pl.ds(first, length)
    total = scaled(train[rows, :], matrix[...], weight[rows, :]).astype(F32)
    for other in got:
        total = total + other[:length, :].astype(F32)
    return store(out, first - at, at, buffer, sems, total / ensemble)


def sum_kernel(ensemble, first, lengths, train, matrix, weight, *rest):
    out, buffer, sems = rest[-3:]
    copies, at, others = [], 0, ensemble - 1
    for i, length in enumerate(lengths):
        got = rest[i * others : (i + 1) * others]
        two = [sems.at[2 * i], sems.at[2 * i + 1]]
        copies += sums(
            ensemble, first + at, at, train, matrix, weight, got, out, buffer, two, length
        )
        at += length
    for copy in copies:
        copy.wait()


def both_kernel(ensemble, masks, outers, batches, me, train, matrix, weight, bucket, *rest):
    features, pieces = rest[:batches], rest[batches : batches + len(masks)]
    out, matrix2, weight2, buffer, sems = rest[-5:]
    count = buffer.shape[0]
    extra = sum(batch.shape[0] for batch in features) - count
    table = jnp.zeros((extra, LANES), F32)
    for part in range(3):
        lanes = pl.ds(part * LANES, LANES)
        table = table + features[0][features[0].shape[0] - extra :, lanes].astype(F32)
    weight2[...] = weights_of(bucket[:, :count], table)
    rows = pieces[0].shape[1]
    for mask, piece in zip(masks, pieces):
        for i, outer in enumerate(outers):
            at = lax.bitwise_xor(me[0], mask ^ outer)
            matrix2[aligned(at, rows), :] = piece[i]
    copies, first = [], 0
    for i, batch in enumerate(features):
        each = batch.shape[0] - (0 if i else extra)
        rows = pl.ds(first, each)
        total = scaled(train[rows, :], matrix[...], weight[rows, :]).astype(F32)
        total = total + scaled(batch[:each, :], matrix2[...], weight2[rows, :]).astype(F32)
        two = [sems.at[2 * i], sems.at[2 * i + 1]]
        copies += store(out, 0, first, buffer, two, total / ensemble)
        first += each
    for copy in copies:
        copy.wait()


def shards(train_feat, test_feat, kernel_inv, bucket_weight, bucket, test_order):
    ensemble, n = lax.axis_size("ckpt"), lax.axis_size("train")
    outer_bits, inner_bits, core_bits = bits_of(n)
    outers = masks_of(outer_bits)
    inners = masks_of(inner_bits + core_bits)
    train = train_feat[0]
    rows, size = train.shape
    count = test_order.shape[0]
    width = count // ensemble
    share = size // n
    unit = rows // 32
    paired = ensemble == 2
    batches = [7, 6] if paired else []
    featured = sum(batches)
    parts = [1, 8, 5, 5] if paired else [16, 16]
    flying = 2
    table_rows = -(-bucket_weight.shape[1] // 16) * 16

    ckpt = lax.axis_index("ckpt").astype(jnp.int32).reshape(1)
    me = lax.axis_index("train").astype(jnp.int32).reshape(1)
    order = test_order.reshape(len(outers), 1, count // len(outers))
    bucket = bucket.reshape(1, rows)

    sent = [shape((part * unit + (0 if i else table_rows), size)) for i, part in enumerate(batches)]
    steps = 2
    own, *features = call(
        functools.partial(start_kernel, steps),
        [shape((2, test_feat.shape[1], size)), *sent],
        (test_feat, kernel_inv, train, bucket_weight), [ANY] * 3 + [VMEM],
        out_specs=[ANY] * (1 + len(sent)), mib=60,
        scratch=[
            pltpu.VMEM((2, test_feat.shape[1], size), BF16),
            pltpu.VMEM((max(featured, 1) * unit, size), BF16),
            pltpu.VMEM((table_rows, size), BF16),
            pltpu.SemaphoreType.DMA((2, 3 + steps * len(sent))),
        ],
    )
    features = [lax.ppermute(batch, "ckpt", ahead(1, ensemble)) for batch in features]

    groups = []
    for mask, block in sorted(spread(own, outer_bits, n), key=lambda e: e[0]):
        held = [(mask, block)]
        inner = spread(block, inner_bits, n, mask)[1:]
        held = spread_on(held + inner, core_bits, n)
        groups.append(([m for m, _ in held], [b for _, b in held]))
    weight = call(
        functools.partial(weights_kernel, table_rows), shape((rows, LANES), F32),
        (bucket, bucket_weight), [VMEM] * 2,
    )

    half = 2 * size * size * width
    state = []
    for masks, blocks in groups[:-1]:
        operands = [ckpt, me, order, *blocks, *state]
        after = features[:1] if not state else []
        state = call(
            functools.partial(part_kernel, ensemble, masks),
            [shape((size, size)), shape((count, size))],
            [*operands, *after], [SMEM] * 2 + [VMEM] * (len(operands) - 2) + [ANY] * len(after),
            scratch=[pltpu.VMEM((count // len(outers), size), BF16)],
            aliases={len(operands) - 2: 0, len(operands) - 1: 1} if state else None,
            flops=4 * half, moved=4 * size * size,
        )
    masks, blocks = groups[-1]
    inverse, chosen, test, matrices = call(
        functools.partial(send_transform_kernel, ensemble, masks),
        [
            shape((size, size)), shape((count, size)), shape((count // len(outers), size)),
            shape((ensemble - 1, size, width)),
        ],
        [ckpt, me, order, *blocks, *state],
        [SMEM] * 2 + [VMEM] * (3 + len(blocks)),
        aliases={3 + len(blocks): 0, 4 + len(blocks): 1},
        flops=3 * half, moved=4 * size * size, mib=12,
    )

    def send(first, part, after):
        got = []
        for k in range(1, ensemble):
            tile = call(
                functools.partial(send_kernel, first * unit, part * unit, k - 1),
                shape((part * unit, width)),
                (train, matrices, weight, *after), [VMEM] * 3 + [ANY] * len(after),
            )
            after = [tile]
            got.append(lax.ppermute(tile, "ckpt", ahead(k, ensemble)))
        return got, after

    starts = [featured + sum(parts[:q]) for q in range(len(parts))]
    received, after = [], []
    if paired:
        tile = call(
            functools.partial(first_kernel, starts[0] * unit, parts[0] * unit),
            shape((parts[0] * unit + share, width)),
            (me, train, matrices, weight), [SMEM] + [VMEM] * 3,
        )
        received.append([lax.ppermute(tile, "ckpt", ahead(1, ensemble))])
        after = [tile]
    for q in range(len(received), min(flying, len(parts))):
        got, after = send(starts[q], parts[q], after)
        received.append(got)
    if paired:
        piece = call(
            functools.partial(tail_kernel, parts[0] * unit), shape((share, width)),
            (*received[0], *after), [VMEM, ANY],
        )
        after = [piece]

    matrix = call(
        functools.partial(own_transform_kernel, ensemble, masks),
        shape((size, width)), (ckpt, me, order, inverse, chosen, test, *after, *features[1:]),
        [SMEM] * 2 + [VMEM] * 4 + [ANY] * (len(after) + len(features[1:])), flops=3 * half, mib=12,
    )
    if paired:
        got, after = send(starts[flying], parts[flying], after)
        received.append(got)
        column = call(
            functools.partial(stack_kernel, len(outers)), shape((len(outers), share, width)),
            [piece] + [swap(piece, mask, n) for mask in outers[1:]] + [matrix],
            [VMEM] * len(outers) + [ANY],
        )
        for q in range(flying + 1, len(parts)):
            got, after = send(starts[q], parts[q], [column])
            received.append(got)
        held = [(0, column)]
        for bit in inner_bits:
            held += [(mask ^ bit, swap(b, bit, n)) for mask, b in held]
        held = held[:1] + [
            (mask, call(relay_kernel, shape(b.shape), (b, *received[1], *received[2]), [VMEM, ANY, ANY]))
            for mask, b in held[1:]
        ]
        for bit in core_bits:
            held += [(mask ^ bit, swap(b, bit, n)) for mask, b in held]
        pieces = [b for _, b in sorted(held, key=lambda entry: entry[0])]

    out = None

    def put(kernel, part, copies, operands, specs, scratch=()):
        held = [] if out is None else [out]
        return call(
            kernel, shape((rows, width), F32),
            (*operands, *held), specs + [ANY] * len(held),
            out_specs=[ANY],
            scratch=[
                *scratch, pltpu.VMEM((part * unit, width), F32), pltpu.SemaphoreType.DMA((copies,)),
            ],
            aliases={len(operands): 0} if held else None, mib=24,
        )

    together = [[0, 1, 2], [], [3]] if paired else [[q] for q in range(len(parts))]
    for chunks in together:
        if chunks:
            part = sum(parts[q] for q in chunks)
            got = [tile for q in chunks for tile in received[q]]
            lengths = [parts[q] * unit for q in chunks]
            out = put(
                functools.partial(sum_kernel, ensemble, starts[chunks[0]] * unit, lengths),
                part, 2 * len(chunks), (train, matrix, weight, *got), [VMEM] * (3 + len(got)),
            )
        else:
            out = put(
                functools.partial(both_kernel, ensemble, inners, outers, len(batches)),
                featured, 2 * len(batches),
                (me, train, matrix, weight, bucket, *features, *pieces),
                [SMEM] + [VMEM] * (4 + len(features) + len(pieces)),
                scratch=[
                    pltpu.VMEM((size, width), BF16), pltpu.VMEM((featured * unit, LANES), F32)
                ],
            )
    return out


def solution(mesh):
    return jax.shard_map(
        shards,
        mesh=mesh,
        in_specs=(
            P("ckpt", "train", None),
            P("ckpt", "train", None),
            P("ckpt", "train", None),
            P("ckpt", None),
            P("train"),
            P(),
        ),
        out_specs=P("train", "ckpt"),
        check_vma=False,
    )
```

```python
import functools
import jax
import jax.numpy as jnp
from jax import lax
from jax.experimental import pallas as pl
from jax.experimental.pallas import tpu as pltpu
from jax.sharding import PartitionSpec as P

VMEM = pl.BlockSpec(memory_space=pltpu.VMEM)
SMEM = pl.BlockSpec(memory_space=pltpu.SMEM)
ANY = pl.BlockSpec(memory_space=pl.ANY)
F32 = jnp.float32
BF16 = jnp.bfloat16
MIB = 1024 * 1024
LANES = 128


def bits_of(n):
    bits = [1 << i for i in reversed(range(n.bit_length() - 1))]
    assert n == 1 << len(bits)
    core = bits[-1:]
    rest = bits[:-1]
    cut = (len(rest) + 1) // 2
    return rest[:cut], rest[cut:], core


def swap(block, mask, n):
    return lax.ppermute(block, "train", [(d ^ mask, d) for d in range(n)])


def spread(block, bits, n, start=0):
    return spread_on([(start, block)], bits, n)


def spread_on(held, bits, n):
    for bit in bits:
        held += [(mask ^ bit, swap(b, bit, n)) for mask, b in held]
    return sorted(held, key=lambda entry: entry[0])


def masks_of(bits):
    masks = [0]
    for bit in bits:
        masks += [mask ^ bit for mask in masks]
    return sorted(masks)


def ahead(k, n):
    return [(d, (d + k) % n) for d in range(n)]


def aligned(index, rows):
    return pl.ds(pl.multiple_of(index * rows, rows), rows)


def call(kernel, outs, operands, specs, mib=8, flops=0, moved=0, scratch=(), aliases=None, out_specs=None):
    several = isinstance(outs, list)
    out_specs = out_specs or [VMEM] * (len(outs) if several else 1)
    return pl.pallas_call(
        kernel,
        out_shape=outs,
        in_specs=specs,
        out_specs=out_specs if several else out_specs[0],
        scratch_shapes=list(scratch),
        input_output_aliases=aliases or {},
        compiler_params=pltpu.CompilerParams(vmem_limit_bytes=mib * MIB),
        cost_estimate=pl.CostEstimate(flops=flops, bytes_accessed=moved, transcendentals=0),
    )(*operands)


def shape(dims, dtype=BF16):
    return jax.ShapeDtypeStruct(dims, dtype)


def table_of(bucket_weight, rows):
    count = bucket_weight.shape[1]
    at = lax.broadcasted_iota(jnp.int32, (rows, count), 0)
    lane = lax.broadcasted_iota(jnp.int32, (rows, count), 1)
    column = jnp.sum(jnp.where(at == lane, bucket_weight, 0.0), axis=1, keepdims=True)
    return jnp.broadcast_to(column, (rows, LANES))


def weights_of(bucket, table):
    onehot = lax.broadcasted_iota(jnp.int32, (table.shape[0], bucket.shape[1]), 0) == bucket
    return lax.dot_general(
        onehot.astype(F32), table, (((0,), (0,)), ((), ())),
        precision=lax.Precision.HIGHEST, preferred_element_type=F32,
    )


def weights_kernel(table_rows, bucket, bucket_weight, out):
    out[...] = weights_of(bucket[...], table_of(bucket_weight[...], table_rows))


def start_kernel(steps, test_feat, kernel_inv, train, bucket_weight, own, *rest):
    batches, (pair, held, below, sems) = rest[:-4], rest[-4:]
    moves = [(test_feat.at[0], pair.at[0], own.at[0]), (kernel_inv.at[0], pair.at[1], own.at[1])]
    count = below.shape[0]
    first = 0
    for i, batch in enumerate(batches):
        step = (batch.shape[0] - (0 if i else count)) // steps
        for i in range(steps):
            span = pl.ds(first + i * step, step)
            moves.append((train.at[span], held.at[span], batch.at[pl.ds(i * step, step)]))
        first += steps * step
    ins = [
        pltpu.make_async_copy(source, middle, sems.at[0, i])
        for i, (source, middle, _) in enumerate(moves)
    ]
    outs = [
        pltpu.make_async_copy(middle, target, sems.at[1, i])
        for i, (_, middle, target) in enumerate(moves)
    ]
    for copy in ins:
        copy.start()
    if batches:
        left = table_of(bucket_weight[...], count)
        for part in range(3):
            term = left.astype(BF16)
            below[:, part * LANES : (part + 1) * LANES] = term
            left = left - term.astype(F32)
        below[:, 3 * LANES :] = jnp.zeros((count, below.shape[1] - 3 * LANES), BF16)
        span = pl.ds(batches[0].shape[0] - count, count)
        outs.append(pltpu.make_async_copy(below, batches[0].at[span], sems.at[1, len(moves)]))
        outs[-1].start()
    for inward, outward in zip(ins, outs):
        inward.wait()
        outward.start()
    for copy in outs:
        copy.wait()


def choose(ensemble, k, outer, ckpt, order, test):
    width = order.shape[0] * order.shape[2] // ensemble
    first = lax.rem(ckpt[0] + k, ensemble) * width
    wanted = lax.broadcasted_iota(jnp.int32, (width, order.shape[2]), 0) + first
    onehot = (wanted == order[outer]).astype(BF16)
    return jnp.dot(onehot, test[...], preferred_element_type=F32).astype(BF16)


def unpack(masks, me, blocks, test, inverse):
    rows = blocks[0].shape[1]
    for mask, block in zip(masks, blocks):
        at = lax.bitwise_xor(me[0], mask)
        test[aligned(lax.rem(at, len(masks)), rows), :] = block[0]
        inverse[aligned(at, rows), :] = block[1]
    return lax.div(lax.bitwise_xor(me[0], masks[0]), len(masks))


def part_kernel(ensemble, masks, ckpt, me, order, *rest):
    blocks = rest[: len(masks)]
    inverse, chosen, test = rest[-3:]
    outer = unpack(masks, me, blocks, test, inverse)
    width = chosen.shape[0] // ensemble
    for j in range(ensemble):
        rows = pl.ds(j * width, width)
        picked = choose(ensemble, j, outer, ckpt, order, test)
        chosen[rows, :] = picked if masks[0] == 0 else chosen[rows, :] + picked


def transformed(inverse, chosen):
    return lax.dot_general(
        inverse[...], chosen, (((1,), (1,)), ((), ())), preferred_element_type=F32
    ).astype(BF16)


def send_transform_kernel(ensemble, masks, ckpt, me, order, *rest):
    blocks = rest[: len(masks)]
    inverse, chosen, test, out, shard = rest[-5:]
    outer = unpack(masks, me, blocks, test, inverse)
    width = chosen.shape[0] // ensemble
    for j in range(1, ensemble):
        picked = choose(ensemble, j, outer, ckpt, order, test)
        out[j - 1] = transformed(inverse, chosen[pl.ds(j * width, width), :] + picked)
    shard[...] = out[0, aligned(me[0], shard.shape[0]), :]


def own_transform_kernel(ensemble, masks, ckpt, me, order, inverse, chosen, test, *rest):
    outer = lax.div(lax.bitwise_xor(me[0], masks[0]), len(masks))
    picked = choose(ensemble, 0, outer, ckpt, order, test)
    rest[-1][...] = transformed(inverse, chosen[: picked.shape[0], :] + picked)


def scaled(train, matrix, weight):
    tile = jnp.dot(train, matrix, preferred_element_type=F32)
    wide = jnp.concatenate([weight] * (tile.shape[1] // weight.shape[1]), axis=1)
    return (tile * wide).astype(BF16)


def send_kernel(first, length, j, train, matrices, weight, *rest):
    rows = pl.ds(first, length)
    rest[-1][:length, :] = scaled(train[rows, :], matrices[j], weight[rows, :])


def relay_kernel(block, *rest):
    rest[-1][...] = block[...]


def stack_kernel(count, *refs):
    for i, ref in enumerate(refs[:count]):
        refs[-1][i] = ref[...]


def store(out, first, at, buffer, sems, tile):
    rows = tile.shape[0] // len(sems)
    copies = []
    for i, sem in enumerate(sems):
        span = pl.ds(at + i * rows, rows)
        buffer[span, :] = tile[i * rows : (i + 1) * rows]
        copies.append(
            pltpu.make_async_copy(buffer.at[span], out.at[pl.ds(first + at + i * rows, rows)], sem)
        )
        copies[-1].start()
    return copies


def sums(ensemble, first, at, train, matrix, weight, got, out, buffer, sems, length):
    rows = pl.ds(first, length)
    total = scaled(train[rows, :], matrix[...], weight[rows, :]).astype(F32)
    for other in got:
        total = total + other[:length, :].astype(F32)
    return store(out, first - at, at, buffer, sems, total / ensemble)


def sum_kernel(ensemble, first, lengths, train, matrix, weight, *rest):
    out, buffer, sems = rest[-3:]
    copies, at, others = [], 0, ensemble - 1
    for i, length in enumerate(lengths):
        got = rest[i * others : (i + 1) * others]
        two = [sems.at[2 * i], sems.at[2 * i + 1]]
        copies += sums(
            ensemble, first + at, at, train, matrix, weight, got, out, buffer, two, length
        )
        at += length
    for copy in copies:
        copy.wait()


def both_kernel(ensemble, masks, outers, batches, me, train, matrix, weight, bucket, *rest):
    features, pieces = rest[:batches], rest[batches : batches + len(masks)]
    out, matrix2, weight2, buffer, sems = rest[-5:]
    count = buffer.shape[0]
    extra = sum(batch.shape[0] for batch in features) - count
    table = jnp.zeros((extra, LANES), F32)
    for part in range(3):
        lanes = pl.ds(part * LANES, LANES)
        table = table + features[0][features[0].shape[0] - extra :, lanes].astype(F32)
    weight2[...] = weights_of(bucket[:, :count], table)
    rows = pieces[0].shape[1]
    for mask, piece in zip(masks, pieces):
        for i, outer in enumerate(outers):
            at = lax.bitwise_xor(me[0], mask ^ outer)
            matrix2[aligned(at, rows), :] = piece[i]
    copies, first = [], 0
    for i, batch in enumerate(features):
        each = batch.shape[0] - (0 if i else extra)
        rows = pl.ds(first, each)
        total = scaled(train[rows, :], matrix[...], weight[rows, :]).astype(F32)
        total = total + scaled(batch[:each, :], matrix2[...], weight2[rows, :]).astype(F32)
        two = [sems.at[2 * i], sems.at[2 * i + 1]]
        copies += store(out, 0, first, buffer, two, total / ensemble)
        first += each
    for copy in copies:
        copy.wait()


def shards(train_feat, test_feat, kernel_inv, bucket_weight, bucket, test_order):
    ensemble, n = lax.axis_size("ckpt"), lax.axis_size("train")
    outer_bits, inner_bits, core_bits = bits_of(n)
    outers = masks_of(outer_bits)
    inners = masks_of(inner_bits + core_bits)
    train = train_feat[0]
    rows, size = train.shape
    count = test_order.shape[0]
    width = count // ensemble
    share = size // n
    unit = rows // 32
    paired = ensemble == 2
    batches = [7, 7] if paired else []
    featured = sum(batches)
    parts = [7, 6, 5] if paired else [16, 16]
    flying = 1 if paired else 2
    table_rows = -(-bucket_weight.shape[1] // 16) * 16

    ckpt = lax.axis_index("ckpt").astype(jnp.int32).reshape(1)
    me = lax.axis_index("train").astype(jnp.int32).reshape(1)
    order = test_order.reshape(len(outers), 1, count // len(outers))
    bucket = bucket.reshape(1, rows)

    sent = [
        shape((part * unit + (0 if i else table_rows), size))
        for i, part in enumerate(batches)
    ]
    steps = 2
    own, *features = call(
        functools.partial(start_kernel, steps),
        [shape((2, test_feat.shape[1], size)), *sent],
        (test_feat, kernel_inv, train, bucket_weight), [ANY] * 3 + [VMEM],
        out_specs=[ANY] * (1 + len(sent)), mib=60,
        scratch=[
            pltpu.VMEM((2, test_feat.shape[1], size), BF16),
            pltpu.VMEM((max(featured, 1) * unit, size), BF16),
            pltpu.VMEM((table_rows, size), BF16),
            pltpu.SemaphoreType.DMA((2, 3 + steps * len(sent))),
        ],
    )
    features = [lax.ppermute(batch, "ckpt", ahead(1, ensemble)) for batch in features]

    groups = []
    for mask, block in sorted(spread(own, outer_bits, n), key=lambda e: e[0]):
        held = [(mask, block)]
        inner = spread(block, inner_bits, n, mask)[1:]
        held = spread_on(held + inner, core_bits, n)
        groups.append(([m for m, _ in held], [b for _, b in held]))
    weight = call(
        functools.partial(weights_kernel, table_rows), shape((rows, LANES), F32),
        (bucket, bucket_weight), [VMEM] * 2,
    )

    half = 2 * size * size * width
    state = []
    for masks, blocks in groups[:-1]:
        operands = [ckpt, me, order, *blocks, *state]
        after = features[:1] if not state else [weight]
        state = call(
            functools.partial(part_kernel, ensemble, masks),
            [shape((size, size)), shape((count, size))],
            [*operands, *after], [SMEM] * 2 + [VMEM] * (len(operands) - 2) + [ANY] * len(after),
            scratch=[pltpu.VMEM((count // len(outers), size), BF16)],
            aliases={len(operands) - 2: 0, len(operands) - 1: 1} if state else None,
            flops=4 * half, moved=4 * size * size,
        )
    masks, blocks = groups[-1]
    starts = [featured + sum(parts[:q]) for q in range(len(parts))]
    inverse, chosen, test, matrices, shard = call(
        functools.partial(send_transform_kernel, ensemble, masks),
        [
            shape((size, size)), shape((count, size)), shape((count // len(outers), size)),
            shape((ensemble - 1, size, width)), shape((share, width)),
        ],
        [ckpt, me, order, *blocks, *state], [SMEM] * 2 + [VMEM] * (3 + len(blocks)),
        aliases={3 + len(blocks): 0, 4 + len(blocks): 1},
        flops=3 * half, moved=4 * size * size, mib=12,
    )

    def send(first, part, after):
        got = []
        for k in range(1, ensemble):
            tile = call(
                functools.partial(send_kernel, first * unit, part * unit, k - 1),
                shape((part * unit, width)),
                (train, matrices, weight, *after), [VMEM] * 3 + [ANY] * len(after),
            )
            after = [tile]
            got.append(lax.ppermute(tile, "ckpt", ahead(k, ensemble)))
        return got, after

    received, after = [], []
    if paired:
        shard2 = lax.ppermute(shard, "ckpt", ahead(1, ensemble))
    for q in range(min(flying, len(parts))):
        got, after = send(starts[q], parts[q], after)
        received.append(got)
    if paired:
        piece = call(relay_kernel, shape(shard2.shape), (shard2, *after), [VMEM, ANY])
        after = [piece]

    matrix = call(
        functools.partial(own_transform_kernel, ensemble, masks),
        shape((size, width)), (ckpt, me, order, inverse, chosen, test, *after, *features[1:]),
        [SMEM] * 2 + [VMEM] * 4 + [ANY] * (len(after) + len(features[1:])), flops=3 * half, mib=12,
    )
    if paired:
        got, after = send(starts[flying], parts[flying], after)
        received.append(got)
        column = call(
            functools.partial(stack_kernel, len(outers)), shape((len(outers), share, width)),
            [piece] + [swap(piece, mask, n) for mask in outers[1:]] + [matrix],
            [VMEM] * len(outers) + [ANY],
        )
        for q in range(flying + 1, len(parts)):
            got, after = send(starts[q], parts[q], [column])
            received.append(got)
        held = [(0, column)]
        for bit in inner_bits:
            held += [(mask ^ bit, swap(b, bit, n)) for mask, b in held]
        held = held[:1] + [
            (mask, call(relay_kernel, shape(b.shape), (b, *received[0], *received[1]), [VMEM, ANY, ANY]))
            for mask, b in held[1:]
        ]
        for bit in core_bits:
            held += [(mask ^ bit, swap(b, bit, n)) for mask, b in held]
        pieces = [b for _, b in sorted(held, key=lambda entry: entry[0])]

    out = None

    def put(kernel, part, copies, operands, specs, scratch=()):
        held = [] if out is None else [out]
        return call(
            kernel, shape((rows, width), F32),
            (*operands, *held), specs + [ANY] * len(held),
            out_specs=[ANY],
            scratch=[
                *scratch, pltpu.VMEM((part * unit, width), F32), pltpu.SemaphoreType.DMA((copies,)),
            ],
            aliases={len(operands): 0} if held else None, mib=24,
        )

    together = [[0, 1], [], [2]] if paired else [[q] for q in range(len(parts))]
    for chunks in together:
        if chunks:
            part = sum(parts[q] for q in chunks)
            got = [tile for q in chunks for tile in received[q]]
            lengths = [parts[q] * unit for q in chunks]
            out = put(
                functools.partial(sum_kernel, ensemble, starts[chunks[0]] * unit, lengths),
                part, 2 * len(chunks), (train, matrix, weight, *got), [VMEM] * (3 + len(got)),
            )
        else:
            out = put(
                functools.partial(both_kernel, ensemble, inners, outers, len(batches)),
                featured, 2 * len(batches),
                (me, train, matrix, weight, bucket, *features, *pieces),
                [SMEM] + [VMEM] * (4 + len(features) + len(pieces)),
                scratch=[
                    pltpu.VMEM((size, width), BF16), pltpu.VMEM((featured * unit, LANES), F32)
                ],
            )
    return out


def solution(mesh):
    return jax.shard_map(
        shards,
        mesh=mesh,
        in_specs=(
            P("ckpt", "train", None),
            P("ckpt", "train", None),
            P("ckpt", "train", None),
            P("ckpt", None),
            P("train"),
            P(),
        ),
        out_specs=P("train", "ckpt"),
        check_vma=False,
    )
```

```python
import functools
import jax
import jax.numpy as jnp
from jax import lax
from jax.experimental import pallas as pl
from jax.experimental.pallas import tpu as pltpu
from jax.sharding import PartitionSpec as P

VMEM = pl.BlockSpec(memory_space=pltpu.VMEM)
SMEM = pl.BlockSpec(memory_space=pltpu.SMEM)
ANY = pl.BlockSpec(memory_space=pl.ANY)
F32 = jnp.float32
BF16 = jnp.bfloat16
MIB = 1024 * 1024
LANES = 128


def bits_of(n):
    bits = [1 << i for i in reversed(range(n.bit_length() - 1))]
    assert n == 1 << len(bits)
    core = bits[-1:]
    rest = bits[:-1]
    cut = (len(rest) + 1) // 2
    return rest[:cut], rest[cut:], core


def swap(block, mask, n):
    return lax.ppermute(block, "train", [(d ^ mask, d) for d in range(n)])


def spread(block, bits, n, start=0):
    return spread_on([(start, block)], bits, n)


def spread_on(held, bits, n):
    for bit in bits:
        held += [(mask ^ bit, swap(b, bit, n)) for mask, b in held]
    return sorted(held, key=lambda entry: entry[0])


def masks_of(bits):
    masks = [0]
    for bit in bits:
        masks += [mask ^ bit for mask in masks]
    return sorted(masks)


def ahead(k, n):
    return [(d, (d + k) % n) for d in range(n)]


def aligned(index, rows):
    return pl.ds(pl.multiple_of(index * rows, rows), rows)


def call(kernel, outs, operands, specs, mib=8, flops=0, moved=0, scratch=(), aliases=None, out_specs=None):
    several = isinstance(outs, list)
    out_specs = out_specs or [VMEM] * (len(outs) if several else 1)
    return pl.pallas_call(
        kernel,
        out_shape=outs,
        in_specs=specs,
        out_specs=out_specs if several else out_specs[0],
        scratch_shapes=list(scratch),
        input_output_aliases=aliases or {},
        compiler_params=pltpu.CompilerParams(vmem_limit_bytes=mib * MIB),
        cost_estimate=pl.CostEstimate(flops=flops, bytes_accessed=moved, transcendentals=0),
    )(*operands)


def shape(dims, dtype=BF16):
    return jax.ShapeDtypeStruct(dims, dtype)


def table_of(bucket_weight, rows):
    count = bucket_weight.shape[1]
    at = lax.broadcasted_iota(jnp.int32, (rows, count), 0)
    lane = lax.broadcasted_iota(jnp.int32, (rows, count), 1)
    column = jnp.sum(jnp.where(at == lane, bucket_weight, 0.0), axis=1, keepdims=True)
    return jnp.broadcast_to(column, (rows, LANES))


def weights_of(bucket, table):
    onehot = lax.broadcasted_iota(jnp.int32, (table.shape[0], bucket.shape[1]), 0) == bucket
    return lax.dot_general(
        onehot.astype(F32), table, (((0,), (0,)), ((), ())),
        precision=lax.Precision.HIGHEST, preferred_element_type=F32,
    )


def weights_kernel(table_rows, bucket, bucket_weight, out):
    out[...] = weights_of(bucket[...], table_of(bucket_weight[...], table_rows))


def start_kernel(steps, test_feat, kernel_inv, train, bucket_weight, own, *rest):
    batches, (pair, held, below, sems) = rest[:-4], rest[-4:]
    moves = [(test_feat.at[0], pair.at[0], own.at[0]), (kernel_inv.at[0], pair.at[1], own.at[1])]
    count = below.shape[0]
    first = 0
    for i, batch in enumerate(batches):
        step = (batch.shape[0] - (0 if i else count)) // steps
        for i in range(steps):
            span = pl.ds(first + i * step, step)
            moves.append((train.at[span], held.at[span], batch.at[pl.ds(i * step, step)]))
        first += steps * step
    ins = [
        pltpu.make_async_copy(source, middle, sems.at[0, i])
        for i, (source, middle, _) in enumerate(moves)
    ]
    outs = [
        pltpu.make_async_copy(middle, target, sems.at[1, i])
        for i, (_, middle, target) in enumerate(moves)
    ]
    for copy in ins:
        copy.start()
    if batches:
        left = table_of(bucket_weight[...], count)
        for part in range(3):
            term = left.astype(BF16)
            below[:, part * LANES : (part + 1) * LANES] = term
            left = left - term.astype(F32)
        below[:, 3 * LANES :] = jnp.zeros((count, below.shape[1] - 3 * LANES), BF16)
        span = pl.ds(batches[0].shape[0] - count, count)
        outs.append(pltpu.make_async_copy(below, batches[0].at[span], sems.at[1, len(moves)]))
        outs[-1].start()
    for inward, outward in zip(ins, outs):
        inward.wait()
        outward.start()
    for copy in outs:
        copy.wait()


def choose(ensemble, k, outer, ckpt, order, test):
    width = order.shape[0] * order.shape[2] // ensemble
    first = lax.rem(ckpt[0] + k, ensemble) * width
    wanted = lax.broadcasted_iota(jnp.int32, (width, order.shape[2]), 0) + first
    onehot = (wanted == order[outer]).astype(BF16)
    return jnp.dot(onehot, test[...], preferred_element_type=F32).astype(BF16)


def unpack(masks, me, blocks, test, inverse):
    rows = blocks[0].shape[1]
    for mask, block in zip(masks, blocks):
        at = lax.bitwise_xor(me[0], mask)
        test[aligned(lax.rem(at, len(masks)), rows), :] = block[0]
        inverse[aligned(at, rows), :] = block[1]
    return lax.div(lax.bitwise_xor(me[0], masks[0]), len(masks))


def part_kernel(ensemble, masks, ckpt, me, order, *rest):
    blocks = rest[: len(masks)]
    inverse, chosen, test = rest[-3:]
    outer = unpack(masks, me, blocks, test, inverse)
    width = chosen.shape[0] // ensemble
    for j in range(ensemble):
        rows = pl.ds(j * width, width)
        picked = choose(ensemble, j, outer, ckpt, order, test)
        chosen[rows, :] = picked if masks[0] == 0 else chosen[rows, :] + picked


def transformed(inverse, chosen):
    return lax.dot_general(
        inverse[...], chosen, (((1,), (1,)), ((), ())), preferred_element_type=F32
    ).astype(BF16)


def send_transform_kernel(ensemble, masks, ckpt, me, order, *rest):
    blocks = rest[: len(masks)]
    inverse, chosen, test, out, shard = rest[-5:]
    outer = unpack(masks, me, blocks, test, inverse)
    width = chosen.shape[0] // ensemble
    for j in range(1, ensemble):
        picked = choose(ensemble, j, outer, ckpt, order, test)
        out[j - 1] = transformed(inverse, chosen[pl.ds(j * width, width), :] + picked)
    shard[...] = out[0, aligned(me[0], shard.shape[0]), :]


def own_transform_kernel(ensemble, masks, ckpt, me, order, inverse, chosen, test, *rest):
    outer = lax.div(lax.bitwise_xor(me[0], masks[0]), len(masks))
    picked = choose(ensemble, 0, outer, ckpt, order, test)
    rest[-1][...] = transformed(inverse, chosen[: picked.shape[0], :] + picked)


def scaled(train, matrix, weight):
    tile = jnp.dot(train, matrix, preferred_element_type=F32)
    wide = jnp.concatenate([weight] * (tile.shape[1] // weight.shape[1]), axis=1)
    return (tile * wide).astype(BF16)


def send_kernel(first, length, j, train, matrices, weight, *rest):
    rows = pl.ds(first, length)
    rest[-1][:length, :] = scaled(train[rows, :], matrices[j], weight[rows, :])


def relay_kernel(block, *rest):
    rest[-1][...] = block[...]


def stack_kernel(count, *refs):
    for i, ref in enumerate(refs[:count]):
        refs[-1][i] = ref[...]


def store(out, first, at, buffer, sems, tile):
    rows = tile.shape[0] // len(sems)
    copies = []
    for i, sem in enumerate(sems):
        span = pl.ds(at + i * rows, rows)
        buffer[span, :] = tile[i * rows : (i + 1) * rows]
        copies.append(
            pltpu.make_async_copy(buffer.at[span], out.at[pl.ds(first + at + i * rows, rows)], sem)
        )
        copies[-1].start()
    return copies


def sums(ensemble, first, at, train, matrix, weight, got, out, buffer, sems, length):
    rows = pl.ds(first, length)
    total = scaled(train[rows, :], matrix[...], weight[rows, :]).astype(F32)
    for other in got:
        total = total + other[:length, :].astype(F32)
    return store(out, first - at, at, buffer, sems, total / ensemble)


def sum_kernel(ensemble, first, lengths, train, matrix, weight, *rest):
    out, buffer, sems = rest[-3:]
    copies, at, others = [], 0, ensemble - 1
    for i, length in enumerate(lengths):
        got = rest[i * others : (i + 1) * others]
        two = [sems.at[2 * i], sems.at[2 * i + 1]]
        copies += sums(
            ensemble, first + at, at, train, matrix, weight, got, out, buffer, two, length
        )
        at += length
    for copy in copies:
        copy.wait()


def ahead_kernel(last, first, train, matrix, weight, bucket, features, _, own, final, weight2):
    count = own.shape[0]
    own[...] = scaled(train[:count, :], matrix[...], weight[:count, :])
    rows = pl.ds(last, final.shape[0])
    final[...] = scaled(train[rows, :], matrix[...], weight[rows, :])
    table = jnp.zeros((features.shape[0] - first, LANES), F32)
    for part in range(3):
        lanes = pl.ds(part * LANES, LANES)
        table = table + features[first:, lanes].astype(F32)
    weight2[...] = weights_of(bucket[:, :count], table)


def last_kernel(ensemble, first, own, *rest):
    out, buffer, sems = rest[-3:]
    total = own[...].astype(F32)
    for other in rest[: ensemble - 1]:
        total = total + other[...].astype(F32)
    two = [sems.at[0], sems.at[1]]
    for copy in store(out, first, 0, buffer, two, total / ensemble):
        copy.wait()


def both_kernel(ensemble, masks, outers, batches, lengths, me, own, weight2, *rest):
    features, pieces = rest[:batches], rest[batches : batches + len(masks)]
    out, matrix2, buffer, sems = rest[-4:]
    rows = pieces[0].shape[1]
    for mask, piece in zip(masks, pieces):
        for i, outer in enumerate(outers):
            at = lax.bitwise_xor(me[0], mask ^ outer)
            matrix2[aligned(at, rows), :] = piece[i]
    copies, first = [], 0
    for i, (batch, each) in enumerate(zip(features, lengths)):
        rows = pl.ds(first, each)
        total = own[rows, :].astype(F32)
        total = total + scaled(batch[:each, :], matrix2[...], weight2[rows, :]).astype(F32)
        two = [sems.at[2 * i], sems.at[2 * i + 1]]
        copies += store(out, 0, first, buffer, two, total / ensemble)
        first += each
    for copy in copies:
        copy.wait()


def shards(train_feat, test_feat, kernel_inv, bucket_weight, bucket, test_order):
    ensemble, n = lax.axis_size("ckpt"), lax.axis_size("train")
    outer_bits, inner_bits, core_bits = bits_of(n)
    outers = masks_of(outer_bits)
    inners = masks_of(inner_bits + core_bits)
    train = train_feat[0]
    rows, size = train.shape
    count = test_order.shape[0]
    width = count // ensemble
    share = size // n
    unit = rows // 64
    paired = ensemble == 2
    batches = [14, 14] if paired else []
    featured = sum(batches)
    parts = [16, 10, 10] if paired else [32, 32]
    flying = 1 if paired else 2
    table_rows = -(-bucket_weight.shape[1] // 16) * 16

    ckpt = lax.axis_index("ckpt").astype(jnp.int32).reshape(1)
    me = lax.axis_index("train").astype(jnp.int32).reshape(1)
    order = test_order.reshape(len(outers), 1, count // len(outers))
    bucket = bucket.reshape(1, rows)

    sent = [
        shape((part * unit + (0 if i else table_rows), size))
        for i, part in enumerate(batches)
    ]
    steps = 2
    own, *features = call(
        functools.partial(start_kernel, steps),
        [shape((2, test_feat.shape[1], size)), *sent],
        (test_feat, kernel_inv, train, bucket_weight), [ANY] * 3 + [VMEM],
        out_specs=[ANY] * (1 + len(sent)), mib=60,
        scratch=[
            pltpu.VMEM((2, test_feat.shape[1], size), BF16),
            pltpu.VMEM((max(featured, 1) * unit, size), BF16),
            pltpu.VMEM((table_rows, size), BF16),
            pltpu.SemaphoreType.DMA((2, 3 + steps * len(sent))),
        ],
    )
    features = [lax.ppermute(batch, "ckpt", ahead(1, ensemble)) for batch in features]

    groups = []
    for mask, block in sorted(spread(own, outer_bits, n), key=lambda e: e[0]):
        held = [(mask, block)]
        inner = spread(block, inner_bits, n, mask)[1:]
        held = spread_on(held + inner, core_bits, n)
        groups.append(([m for m, _ in held], [b for _, b in held]))
    weight = call(
        functools.partial(weights_kernel, table_rows), shape((rows, LANES), F32),
        (bucket, bucket_weight), [VMEM] * 2,
    )

    half = 2 * size * size * width
    state = []
    for masks, blocks in groups[:-1]:
        operands = [ckpt, me, order, *blocks, *state]
        after = features[:1] if not state else [weight]
        state = call(
            functools.partial(part_kernel, ensemble, masks),
            [shape((size, size)), shape((count, size))],
            [*operands, *after], [SMEM] * 2 + [VMEM] * (len(operands) - 2) + [ANY] * len(after),
            scratch=[pltpu.VMEM((count // len(outers), size), BF16)],
            aliases={len(operands) - 2: 0, len(operands) - 1: 1} if state else None,
            flops=4 * half, moved=4 * size * size,
        )
    masks, blocks = groups[-1]
    starts = [featured + sum(parts[:q]) for q in range(len(parts))]
    inverse, chosen, test, matrices, shard = call(
        functools.partial(send_transform_kernel, ensemble, masks),
        [
            shape((size, size)), shape((count, size)), shape((count // len(outers), size)),
            shape((ensemble - 1, size, width)), shape((share, width)),
        ],
        [ckpt, me, order, *blocks, *state], [SMEM] * 2 + [VMEM] * (3 + len(blocks)),
        aliases={3 + len(blocks): 0, 4 + len(blocks): 1},
        flops=3 * half, moved=4 * size * size, mib=12,
    )

    def send(first, part, after):
        got = []
        for k in range(1, ensemble):
            tile = call(
                functools.partial(send_kernel, first * unit, part * unit, k - 1),
                shape((part * unit, width)),
                (train, matrices, weight, *after), [VMEM] * 3 + [ANY] * len(after),
            )
            after = [tile]
            got.append(lax.ppermute(tile, "ckpt", ahead(k, ensemble)))
        return got, after

    received, after = [], []
    if paired:
        shard2 = lax.ppermute(shard, "ckpt", ahead(1, ensemble))
    for q in range(min(flying, len(parts))):
        got, after = send(starts[q], parts[q], after)
        received.append(got)
    if paired:
        piece = call(relay_kernel, shape(shard2.shape), (shard2, *after), [VMEM, ANY])
        after = [piece]

    matrix = call(
        functools.partial(own_transform_kernel, ensemble, masks),
        shape((size, width)), (ckpt, me, order, inverse, chosen, test, *after, *features[1:]),
        [SMEM] * 2 + [VMEM] * 4 + [ANY] * (len(after) + len(features[1:])), flops=3 * half, mib=12,
    )
    if paired:
        got, after = send(starts[flying], parts[flying], after)
        received.append(got)
        column = call(
            functools.partial(stack_kernel, len(outers)), shape((len(outers), share, width)),
            [piece] + [swap(piece, mask, n) for mask in outers[1:]] + [matrix],
            [VMEM] * len(outers) + [ANY],
        )
        for q in range(flying + 1, len(parts)):
            got, after = send(starts[q], parts[q], [column])
            received.append(got)
        own_rows, last_rows, weight2 = call(
            functools.partial(ahead_kernel, starts[-1] * unit, batches[0] * unit),
            [
                shape((featured * unit, width)), shape((parts[-1] * unit, width)),
                shape((featured * unit, LANES), F32),
            ],
            (train, matrix, weight, bucket, features[0], column), [VMEM] * 5 + [ANY], mib=16,
        )
        held = [(0, column)]
        for bit in inner_bits:
            held += [(mask ^ bit, swap(b, bit, n)) for mask, b in held]
        held = held[:1] + [
            (mask, call(relay_kernel, shape(b.shape), (b, *received[0], *received[1], own_rows), [VMEM] + [ANY] * 3))
            for mask, b in held[1:]
        ]
        for bit in core_bits:
            held += [(mask ^ bit, swap(b, bit, n)) for mask, b in held]
        pieces = [b for _, b in sorted(held, key=lambda entry: entry[0])]

    out = None

    def put(kernel, part, copies, operands, specs, scratch=()):
        held = [] if out is None else [out]
        return call(
            kernel, shape((rows, width), F32),
            (*operands, *held), specs + [ANY] * len(held),
            out_specs=[ANY],
            scratch=[
                *scratch, pltpu.VMEM((part * unit, width), F32), pltpu.SemaphoreType.DMA((copies,)),
            ],
            aliases={len(operands): 0} if held else None, mib=24,
        )

    together = [[0, 1], [], [2]] if paired else [[q] for q in range(len(parts))]
    for chunks in together:
        part = sum(parts[q] for q in chunks)
        got = [tile for q in chunks for tile in received[q]]
        if paired and not chunks:
            lengths = [part * unit for part in batches]
            out = put(
                functools.partial(both_kernel, ensemble, inners, outers, len(batches), lengths),
                featured, 2 * len(batches), (me, own_rows, weight2, *features, *pieces),
                [SMEM] + [VMEM] * (2 + len(features) + len(pieces)),
                scratch=[pltpu.VMEM((size, width), BF16)],
            )
        elif paired and chunks == together[-1]:
            out = put(
                functools.partial(last_kernel, ensemble, starts[chunks[0]] * unit),
                part, 2, (last_rows, *got), [VMEM] * (1 + len(got)),
            )
        else:
            lengths = [parts[q] * unit for q in chunks]
            out = put(
                functools.partial(sum_kernel, ensemble, starts[chunks[0]] * unit, lengths),
                part, 2 * len(chunks), (train, matrix, weight, *got), [VMEM] * (3 + len(got)),
            )
    return out


def solution(mesh):
    return jax.shard_map(
        shards,
        mesh=mesh,
        in_specs=(
            P("ckpt", "train", None),
            P("ckpt", "train", None),
            P("ckpt", "train", None),
            P("ckpt", None),
            P("train"),
            P(),
        ),
        out_specs=P("train", "ckpt"),
        check_vma=False,
    )
```

```python
import functools
import jax
import jax.numpy as jnp
from jax import lax
from jax.experimental import pallas as pl
from jax.experimental.pallas import tpu as pltpu
from jax.sharding import PartitionSpec as P

VMEM = pl.BlockSpec(memory_space=pltpu.VMEM)
SMEM = pl.BlockSpec(memory_space=pltpu.SMEM)
ANY = pl.BlockSpec(memory_space=pl.ANY)
F32 = jnp.float32
BF16 = jnp.bfloat16
MIB = 1024 * 1024
LANES = 128


def bits_of(n):
    bits = [1 << i for i in reversed(range(n.bit_length() - 1))]
    assert n == 1 << len(bits)
    core = bits[-1:]
    rest = bits[:-1]
    cut = (len(rest) + 1) // 2
    return rest[:cut], rest[cut:], core


def swap(block, mask, n):
    return lax.ppermute(block, "train", [(d ^ mask, d) for d in range(n)])


def spread(block, bits, n, start=0):
    return spread_on([(start, block)], bits, n)


def spread_on(held, bits, n):
    for bit in bits:
        held += [(mask ^ bit, swap(b, bit, n)) for mask, b in held]
    return sorted(held, key=lambda entry: entry[0])


def masks_of(bits):
    masks = [0]
    for bit in bits:
        masks += [mask ^ bit for mask in masks]
    return sorted(masks)


def ahead(k, n):
    return [(d, (d + k) % n) for d in range(n)]


def aligned(index, rows):
    return pl.ds(pl.multiple_of(index * rows, rows), rows)


def call(kernel, outs, operands, specs, mib=8, flops=0, moved=0, scratch=(), aliases=None, out_specs=None):
    several = isinstance(outs, list)
    out_specs = out_specs or [VMEM] * (len(outs) if several else 1)
    return pl.pallas_call(
        kernel,
        out_shape=outs,
        in_specs=specs,
        out_specs=out_specs if several else out_specs[0],
        scratch_shapes=list(scratch),
        input_output_aliases=aliases or {},
        compiler_params=pltpu.CompilerParams(vmem_limit_bytes=mib * MIB),
        cost_estimate=pl.CostEstimate(flops=flops, bytes_accessed=moved, transcendentals=0),
    )(*operands)


def shape(dims, dtype=BF16):
    return jax.ShapeDtypeStruct(dims, dtype)


def table_of(bucket_weight, rows):
    count = bucket_weight.shape[1]
    at = lax.broadcasted_iota(jnp.int32, (rows, count), 0)
    lane = lax.broadcasted_iota(jnp.int32, (rows, count), 1)
    column = jnp.sum(jnp.where(at == lane, bucket_weight, 0.0), axis=1, keepdims=True)
    return jnp.broadcast_to(column, (rows, LANES))


def weights_of(bucket, table):
    onehot = lax.broadcasted_iota(jnp.int32, (table.shape[0], bucket.shape[1]), 0) == bucket
    return lax.dot_general(
        onehot.astype(F32), table, (((0,), (0,)), ((), ())),
        precision=lax.Precision.HIGHEST, preferred_element_type=F32,
    )


def weights_kernel(table_rows, bucket, bucket_weight, out):
    out[...] = weights_of(bucket[...], table_of(bucket_weight[...], table_rows))


def start_kernel(steps, test_feat, kernel_inv, train, own, *rest):
    batches, (pair, held, sems) = rest[:-3], rest[-3:]
    moves = [(test_feat.at[0], pair.at[0], own.at[0]), (kernel_inv.at[0], pair.at[1], own.at[1])]
    first = 0
    for batch in batches:
        step = batch.shape[0] // steps
        for i in range(steps):
            span = pl.ds(first + i * step, step)
            moves.append((train.at[span], held.at[span], batch.at[pl.ds(i * step, step)]))
        first += steps * step
    ins = [
        pltpu.make_async_copy(source, middle, sems.at[0, i])
        for i, (source, middle, _) in enumerate(moves)
    ]
    outs = [
        pltpu.make_async_copy(middle, target, sems.at[1, i])
        for i, (_, middle, target) in enumerate(moves)
    ]
    for copy in ins:
        copy.start()
    for inward, outward in zip(ins, outs):
        inward.wait()
        outward.start()
    for copy in outs:
        copy.wait()


def choose(ensemble, k, outer, ckpt, order, test):
    width = order.shape[0] * order.shape[2] // ensemble
    first = lax.rem(ckpt[0] + k, ensemble) * width
    wanted = lax.broadcasted_iota(jnp.int32, (width, order.shape[2]), 0) + first
    onehot = (wanted == order[outer]).astype(BF16)
    return jnp.dot(onehot, test[...], preferred_element_type=F32).astype(BF16)


def unpack(masks, me, blocks, test, inverse):
    rows = blocks[0].shape[1]
    for mask, block in zip(masks, blocks):
        at = lax.bitwise_xor(me[0], mask)
        test[aligned(lax.rem(at, len(masks)), rows), :] = block[0]
        inverse[aligned(at, rows), :] = block[1]
    return lax.div(lax.bitwise_xor(me[0], masks[0]), len(masks))


def part_kernel(ensemble, masks, ckpt, me, order, *rest):
    blocks = rest[: len(masks)]
    inverse, chosen, test = rest[-3:]
    outer = unpack(masks, me, blocks, test, inverse)
    width = chosen.shape[0] // ensemble
    for j in range(ensemble):
        rows = pl.ds(j * width, width)
        picked = choose(ensemble, j, outer, ckpt, order, test)
        chosen[rows, :] = picked if masks[0] == 0 else chosen[rows, :] + picked


def transformed(inverse, chosen):
    return lax.dot_general(
        inverse[...], chosen, (((1,), (1,)), ((), ())), preferred_element_type=F32
    ).astype(BF16)


def send_transform_kernel(ensemble, masks, share, ckpt, me, order, bucket_weight, *rest):
    blocks = rest[: len(masks)]
    inverse, chosen, test, out, shard = rest[-5:]
    outer = unpack(masks, me, blocks, test, inverse)
    width = chosen.shape[0] // ensemble
    for j in range(1, ensemble):
        picked = choose(ensemble, j, outer, ckpt, order, test)
        out[j - 1] = transformed(inverse, chosen[pl.ds(j * width, width), :] + picked)
    shard[:share, :] = out[0, aligned(me[0], share), :]
    left = table_of(bucket_weight[...], shard.shape[0] - share)
    for part in range(shard.shape[1] // LANES):
        term = left.astype(BF16)
        shard[share:, part * LANES : (part + 1) * LANES] = term
        left = left - term.astype(F32)


def own_transform_kernel(ensemble, masks, ckpt, me, order, inverse, chosen, test, *rest):
    outer = lax.div(lax.bitwise_xor(me[0], masks[0]), len(masks))
    picked = choose(ensemble, 0, outer, ckpt, order, test)
    rest[-1][...] = transformed(inverse, chosen[: picked.shape[0], :] + picked)


def scaled(train, matrix, weight):
    tile = jnp.dot(train, matrix, preferred_element_type=F32)
    wide = jnp.concatenate([weight] * (tile.shape[1] // weight.shape[1]), axis=1)
    return (tile * wide).astype(BF16)


def send_kernel(first, length, j, train, matrices, weight, *rest):
    rows = pl.ds(first, length)
    rest[-1][:length, :] = scaled(train[rows, :], matrices[j], weight[rows, :])


def head_kernel(block, *rest):
    rest[-1][...] = block[: rest[-1].shape[0], :]


def relay_kernel(block, *rest):
    rest[-1][...] = block[...]


def stack_kernel(count, *refs):
    for i, ref in enumerate(refs[:count]):
        refs[-1][i] = ref[...]


def store(out, first, at, buffer, sems, tile):
    rows = tile.shape[0] // len(sems)
    copies = []
    for i, sem in enumerate(sems):
        span = pl.ds(at + i * rows, rows)
        buffer[span, :] = tile[i * rows : (i + 1) * rows]
        copies.append(
            pltpu.make_async_copy(buffer.at[span], out.at[pl.ds(first + at + i * rows, rows)], sem)
        )
        copies[-1].start()
    return copies


def sums(ensemble, first, at, train, matrix, weight, got, out, buffer, sems, length):
    rows = pl.ds(first, length)
    total = scaled(train[rows, :], matrix[...], weight[rows, :]).astype(F32)
    for other in got:
        total = total + other[:length, :].astype(F32)
    return store(out, first - at, at, buffer, sems, total / ensemble)


def sum_kernel(ensemble, first, lengths, train, matrix, weight, *rest):
    out, buffer, sems = rest[-3:]
    copies, at, others = [], 0, ensemble - 1
    for i, length in enumerate(lengths):
        got = rest[i * others : (i + 1) * others]
        two = [sems.at[2 * i], sems.at[2 * i + 1]]
        copies += sums(
            ensemble, first + at, at, train, matrix, weight, got, out, buffer, two, length
        )
        at += length
    for copy in copies:
        copy.wait()


def ahead_kernel(last, first, train, matrix, weight, bucket, shared, _, own, final, weight2):
    count = own.shape[0]
    own[...] = scaled(train[:count, :], matrix[...], weight[:count, :])
    rows = pl.ds(last, final.shape[0])
    final[...] = scaled(train[rows, :], matrix[...], weight[rows, :])
    table = jnp.zeros((shared.shape[0] - first, LANES), F32)
    for part in range(3):
        lanes = pl.ds(part * LANES, LANES)
        table = table + shared[first:, lanes].astype(F32)
    weight2[...] = weights_of(bucket[:, :count], table)


def last_kernel(ensemble, first, own, *rest):
    out, buffer, sems = rest[-3:]
    total = own[...].astype(F32)
    for other in rest[: ensemble - 1]:
        total = total + other[...].astype(F32)
    two = [sems.at[0], sems.at[1]]
    for copy in store(out, first, 0, buffer, two, total / ensemble):
        copy.wait()


def both_kernel(ensemble, masks, outers, batches, lengths, me, own, weight2, *rest):
    features, pieces = rest[:batches], rest[batches : batches + len(masks)]
    out, matrix2, buffer, sems = rest[-4:]
    rows = pieces[0].shape[1]
    for mask, piece in zip(masks, pieces):
        for i, outer in enumerate(outers):
            at = lax.bitwise_xor(me[0], mask ^ outer)
            matrix2[aligned(at, rows), :] = piece[i]
    copies, first = [], 0
    for i, (batch, each) in enumerate(zip(features, lengths)):
        rows = pl.ds(first, each)
        total = own[rows, :].astype(F32)
        total = total + scaled(batch[:each, :], matrix2[...], weight2[rows, :]).astype(F32)
        two = [sems.at[2 * i], sems.at[2 * i + 1]]
        copies += store(out, 0, first, buffer, two, total / ensemble)
        first += each
    for copy in copies:
        copy.wait()


def shards(train_feat, test_feat, kernel_inv, bucket_weight, bucket, test_order):
    ensemble, n = lax.axis_size("ckpt"), lax.axis_size("train")
    outer_bits, inner_bits, core_bits = bits_of(n)
    outers = masks_of(outer_bits)
    inners = masks_of(inner_bits + core_bits)
    train = train_feat[0]
    rows, size = train.shape
    count = test_order.shape[0]
    width = count // ensemble
    share = size // n
    unit = rows // 64
    paired = ensemble == 2 and width >= 3 * LANES
    batches = [14, 14] if paired else []
    featured = sum(batches)
    parts = [16, 10, 10] if paired else [32, 32]
    flying = 1 if paired else 2
    table_rows = -(-bucket_weight.shape[1] // 16) * 16

    ckpt = lax.axis_index("ckpt").astype(jnp.int32).reshape(1)
    me = lax.axis_index("train").astype(jnp.int32).reshape(1)
    order = test_order.reshape(len(outers), 1, count // len(outers))
    bucket = bucket.reshape(1, rows)

    sent = [
        shape((part * unit, size))
        for part in batches
    ]
    steps = 2
    own, *features = call(
        functools.partial(start_kernel, steps),
        [shape((2, test_feat.shape[1], size)), *sent],
        (test_feat, kernel_inv, train), [ANY] * 3,
        out_specs=[ANY] * (1 + len(sent)), mib=60,
        scratch=[
            pltpu.VMEM((2, test_feat.shape[1], size), BF16),
            pltpu.VMEM((max(featured, 1) * unit, size), BF16),
            pltpu.SemaphoreType.DMA((2, 3 + steps * len(sent))),
        ],
    )
    features = [lax.ppermute(batch, "ckpt", ahead(1, ensemble)) for batch in features]

    groups = []
    for mask, block in sorted(spread(own, outer_bits, n), key=lambda e: e[0]):
        held = [(mask, block)]
        inner = spread(block, inner_bits, n, mask)[1:]
        held = spread_on(held + inner, core_bits, n)
        groups.append(([m for m, _ in held], [b for _, b in held]))
    weight = call(
        functools.partial(weights_kernel, table_rows), shape((rows, LANES), F32),
        (bucket, bucket_weight), [VMEM] * 2,
    )

    half = 2 * size * size * width
    state = []
    for masks, blocks in groups[:-1]:
        operands = [ckpt, me, order, *blocks, *state]
        after = features[:1] if not state else [weight]
        state = call(
            functools.partial(part_kernel, ensemble, masks),
            [shape((size, size)), shape((count, size))],
            [*operands, *after], [SMEM] * 2 + [VMEM] * (len(operands) - 2) + [ANY] * len(after),
            scratch=[pltpu.VMEM((count // len(outers), size), BF16)],
            aliases={len(operands) - 2: 0, len(operands) - 1: 1} if state else None,
            flops=4 * half, moved=4 * size * size,
        )
    masks, blocks = groups[-1]
    starts = [featured + sum(parts[:q]) for q in range(len(parts))]
    inverse, chosen, test, matrices, shard = call(
        functools.partial(send_transform_kernel, ensemble, masks, share),
        [
            shape((size, size)), shape((count, size)), shape((count // len(outers), size)),
            shape((ensemble - 1, size, width)), shape((share + table_rows, width)),
        ],
        [ckpt, me, order, bucket_weight, *blocks, *state],
        [SMEM] * 2 + [VMEM] * (4 + len(blocks)),
        aliases={4 + len(blocks): 0, 5 + len(blocks): 1},
        flops=3 * half, moved=4 * size * size, mib=12,
    )

    def send(first, part, after):
        got = []
        for k in range(1, ensemble):
            tile = call(
                functools.partial(send_kernel, first * unit, part * unit, k - 1),
                shape((part * unit, width)),
                (train, matrices, weight, *after), [VMEM] * 3 + [ANY] * len(after),
            )
            after = [tile]
            got.append(lax.ppermute(tile, "ckpt", ahead(k, ensemble)))
        return got, after

    received, after = [], []
    if paired:
        shard2 = lax.ppermute(shard, "ckpt", ahead(1, ensemble))
    for q in range(min(flying, len(parts))):
        got, after = send(starts[q], parts[q], after)
        received.append(got)
    if paired:
        piece = call(head_kernel, shape((share, width)), (shard2, *after), [VMEM, ANY])
        after = [piece]

    matrix = call(
        functools.partial(own_transform_kernel, ensemble, masks),
        shape((size, width)), (ckpt, me, order, inverse, chosen, test, *after, *features[1:]),
        [SMEM] * 2 + [VMEM] * 4 + [ANY] * (len(after) + len(features[1:])), flops=3 * half, mib=12,
    )
    if paired:
        got, after = send(starts[flying], parts[flying], after)
        received.append(got)
        column = call(
            functools.partial(stack_kernel, len(outers)), shape((len(outers), share, width)),
            [piece] + [swap(piece, mask, n) for mask in outers[1:]] + [matrix],
            [VMEM] * len(outers) + [ANY],
        )
        for q in range(flying + 1, len(parts)):
            got, after = send(starts[q], parts[q], [column])
            received.append(got)
        own_rows, last_rows, weight2 = call(
            functools.partial(ahead_kernel, starts[-1] * unit, share),
            [
                shape((featured * unit, width)), shape((parts[-1] * unit, width)),
                shape((featured * unit, LANES), F32),
            ],
            (train, matrix, weight, bucket, shard2, column), [VMEM] * 5 + [ANY], mib=16,
        )
        held = [(0, column)]
        for bit in inner_bits:
            held += [(mask ^ bit, swap(b, bit, n)) for mask, b in held]
        held = held[:1] + [
            (mask, call(relay_kernel, shape(b.shape), (b, *received[0], *received[1], own_rows), [VMEM] + [ANY] * 3))
            for mask, b in held[1:]
        ]
        for bit in core_bits:
            held += [(mask ^ bit, swap(b, bit, n)) for mask, b in held]
        pieces = [b for _, b in sorted(held, key=lambda entry: entry[0])]

    out = None

    def put(kernel, part, copies, operands, specs, scratch=()):
        held = [] if out is None else [out]
        return call(
            kernel, shape((rows, width), F32),
            (*operands, *held), specs + [ANY] * len(held),
            out_specs=[ANY],
            scratch=[
                *scratch, pltpu.VMEM((part * unit, width), F32), pltpu.SemaphoreType.DMA((copies,)),
            ],
            aliases={len(operands): 0} if held else None, mib=24,
        )

    together = [[0, 1], [], [2]] if paired else [[q] for q in range(len(parts))]
    for chunks in together:
        part = sum(parts[q] for q in chunks)
        got = [tile for q in chunks for tile in received[q]]
        if paired and not chunks:
            lengths = [part * unit for part in batches]
            out = put(
                functools.partial(both_kernel, ensemble, inners, outers, len(batches), lengths),
                featured, 2 * len(batches), (me, own_rows, weight2, *features, *pieces),
                [SMEM] + [VMEM] * (2 + len(features) + len(pieces)),
                scratch=[pltpu.VMEM((size, width), BF16)],
            )
        elif paired and chunks == together[-1]:
            out = put(
                functools.partial(last_kernel, ensemble, starts[chunks[0]] * unit),
                part, 2, (last_rows, *got), [VMEM] * (1 + len(got)),
            )
        else:
            lengths = [parts[q] * unit for q in chunks]
            out = put(
                functools.partial(sum_kernel, ensemble, starts[chunks[0]] * unit, lengths),
                part, 2 * len(chunks), (train, matrix, weight, *got), [VMEM] * (3 + len(got)),
            )
    return out


def solution(mesh):
    return jax.shard_map(
        shards,
        mesh=mesh,
        in_specs=(
            P("ckpt", "train", None),
            P("ckpt", "train", None),
            P("ckpt", "train", None),
            P("ckpt", None),
            P("train"),
            P(),
        ),
        out_specs=P("train", "ckpt"),
        check_vma=False,
    )
```

```python
import functools
import jax
import jax.numpy as jnp
from jax import lax
from jax.experimental import pallas as pl
from jax.experimental.pallas import tpu as pltpu
from jax.sharding import PartitionSpec as P

VMEM = pl.BlockSpec(memory_space=pltpu.VMEM)
SMEM = pl.BlockSpec(memory_space=pltpu.SMEM)
ANY = pl.BlockSpec(memory_space=pl.ANY)
F32 = jnp.float32
BF16 = jnp.bfloat16
MIB = 1024 * 1024
LANES = 128


def bits_of(n):
    bits = [1 << i for i in reversed(range(n.bit_length() - 1))]
    assert n == 1 << len(bits)
    core = bits[-1:]
    rest = bits[:-1]
    cut = (len(rest) + 1) // 2
    return rest[:cut], rest[cut:], core


def swap(block, mask, n):
    return lax.ppermute(block, "train", [(d ^ mask, d) for d in range(n)])


def spread(block, bits, n, start=0):
    return spread_on([(start, block)], bits, n)


def spread_on(held, bits, n):
    for bit in bits:
        held += [(mask ^ bit, swap(b, bit, n)) for mask, b in held]
    return sorted(held, key=lambda entry: entry[0])


def masks_of(bits):
    masks = [0]
    for bit in bits:
        masks += [mask ^ bit for mask in masks]
    return sorted(masks)


def ahead(k, n):
    return [(d, (d + k) % n) for d in range(n)]


def aligned(index, rows):
    return pl.ds(pl.multiple_of(index * rows, rows), rows)


def call(kernel, outs, operands, specs, mib=8, flops=0, moved=0, scratch=(), aliases=None, out_specs=None):
    several = isinstance(outs, list)
    out_specs = out_specs or [VMEM] * (len(outs) if several else 1)
    return pl.pallas_call(
        kernel,
        out_shape=outs,
        in_specs=specs,
        out_specs=out_specs if several else out_specs[0],
        scratch_shapes=list(scratch),
        input_output_aliases=aliases or {},
        compiler_params=pltpu.CompilerParams(vmem_limit_bytes=mib * MIB),
        cost_estimate=pl.CostEstimate(flops=flops, bytes_accessed=moved, transcendentals=0),
    )(*operands)


def shape(dims, dtype=BF16):
    return jax.ShapeDtypeStruct(dims, dtype)


def table_of(bucket_weight, rows):
    count = bucket_weight.shape[1]
    at = lax.broadcasted_iota(jnp.int32, (rows, count), 0)
    lane = lax.broadcasted_iota(jnp.int32, (rows, count), 1)
    column = jnp.sum(jnp.where(at == lane, bucket_weight, 0.0), axis=1, keepdims=True)
    return jnp.broadcast_to(column, (rows, LANES))


def weights_of(bucket, table):
    onehot = lax.broadcasted_iota(jnp.int32, (table.shape[0], bucket.shape[1]), 0) == bucket
    return lax.dot_general(
        onehot.astype(F32), table, (((0,), (0,)), ((), ())),
        precision=lax.Precision.HIGHEST, preferred_element_type=F32,
    )


def weights_kernel(table_rows, bucket, bucket_weight, out):
    out[...] = weights_of(bucket[...], table_of(bucket_weight[...], table_rows))


def start_kernel(steps, test_feat, kernel_inv, train, own, *rest):
    batches, (pair, held, sems) = rest[:-3], rest[-3:]
    moves = [(test_feat.at[0], pair.at[0], own.at[0]), (kernel_inv.at[0], pair.at[1], own.at[1])]
    first = 0
    for batch in batches:
        step = batch.shape[0] // steps
        for i in range(steps):
            span = pl.ds(first + i * step, step)
            moves.append((train.at[span], held.at[span], batch.at[pl.ds(i * step, step)]))
        first += steps * step
    ins = [
        pltpu.make_async_copy(source, middle, sems.at[0, i])
        for i, (source, middle, _) in enumerate(moves)
    ]
    outs = [
        pltpu.make_async_copy(middle, target, sems.at[1, i])
        for i, (_, middle, target) in enumerate(moves)
    ]
    for copy in ins:
        copy.start()
    for inward, outward in zip(ins, outs):
        inward.wait()
        outward.start()
    for copy in outs:
        copy.wait()


def choose(ensemble, k, outer, ckpt, order, test):
    width = order.shape[0] * order.shape[2] // ensemble
    first = lax.rem(ckpt[0] + k, ensemble) * width
    wanted = lax.broadcasted_iota(jnp.int32, (width, order.shape[2]), 0) + first
    onehot = (wanted == order[outer]).astype(BF16)
    return jnp.dot(onehot, test[...], preferred_element_type=F32).astype(BF16)


def unpack(masks, me, blocks, test, inverse):
    rows = blocks[0].shape[1]
    for mask, block in zip(masks, blocks):
        at = lax.bitwise_xor(me[0], mask)
        test[aligned(lax.rem(at, len(masks)), rows), :] = block[0]
        inverse[aligned(at, rows), :] = block[1]
    return lax.div(lax.bitwise_xor(me[0], masks[0]), len(masks))


def part_kernel(ensemble, masks, ckpt, me, order, *rest):
    blocks = rest[: len(masks)]
    inverse, chosen, test = rest[-3:]
    outer = unpack(masks, me, blocks, test, inverse)
    width = chosen.shape[0] // ensemble
    for j in range(ensemble):
        rows = pl.ds(j * width, width)
        picked = choose(ensemble, j, outer, ckpt, order, test)
        chosen[rows, :] = picked if masks[0] == 0 else chosen[rows, :] + picked


def transformed(inverse, chosen):
    return lax.dot_general(
        inverse[...], chosen, (((1,), (1,)), ((), ())), preferred_element_type=F32
    ).astype(BF16)


def send_transform_kernel(ensemble, masks, share, ckpt, me, order, bucket_weight, *rest):
    blocks = rest[: len(masks)]
    inverse, chosen, test, out, shard = rest[-5:]
    outer = unpack(masks, me, blocks, test, inverse)
    width = chosen.shape[0] // ensemble
    for j in range(1, ensemble):
        picked = choose(ensemble, j, outer, ckpt, order, test)
        out[j - 1] = transformed(inverse, chosen[pl.ds(j * width, width), :] + picked)
    shard[:share, :] = out[0, aligned(me[0], share), :]
    left = table_of(bucket_weight[...], shard.shape[0] - share)
    for part in range(shard.shape[1] // LANES):
        term = left.astype(BF16)
        shard[share:, part * LANES : (part + 1) * LANES] = term
        left = left - term.astype(F32)


def own_transform_kernel(ensemble, masks, ckpt, me, order, inverse, chosen, test, *rest):
    outer = lax.div(lax.bitwise_xor(me[0], masks[0]), len(masks))
    picked = choose(ensemble, 0, outer, ckpt, order, test)
    rest[-1][...] = transformed(inverse, chosen[: picked.shape[0], :] + picked)


def scaled(train, matrix, weight):
    tile = jnp.dot(train, matrix, preferred_element_type=F32)
    wide = jnp.concatenate([weight] * (tile.shape[1] // weight.shape[1]), axis=1)
    return (tile * wide).astype(BF16)


def send_kernel(first, length, j, train, matrices, weight, *rest):
    rows = pl.ds(first, length)
    rest[-1][:length, :] = scaled(train[rows, :], matrices[j], weight[rows, :])


def head_kernel(block, *rest):
    rest[-1][...] = block[: rest[-1].shape[0], :]


def relay_kernel(block, *rest):
    rest[-1][...] = block[...]


def stack_kernel(count, *refs):
    for i, ref in enumerate(refs[:count]):
        refs[-1][i] = ref[...]


def store(out, first, at, buffer, sems, tile):
    rows = tile.shape[0] // len(sems)
    copies = []
    for i, sem in enumerate(sems):
        span = pl.ds(at + i * rows, rows)
        buffer[span, :] = tile[i * rows : (i + 1) * rows]
        copies.append(
            pltpu.make_async_copy(buffer.at[span], out.at[pl.ds(first + at + i * rows, rows)], sem)
        )
        copies[-1].start()
    return copies


def sums(ensemble, first, at, train, matrix, weight, got, out, buffer, sems, length):
    rows = pl.ds(first, length)
    total = scaled(train[rows, :], matrix[...], weight[rows, :]).astype(F32)
    for other in got:
        total = total + other[:length, :].astype(F32)
    return store(out, first - at, at, buffer, sems, total / ensemble)


def sum_kernel(ensemble, first, lengths, train, matrix, weight, *rest):
    out, buffer, sems = rest[-3:]
    copies, at, others = [], 0, ensemble - 1
    for i, length in enumerate(lengths):
        got = rest[i * others : (i + 1) * others]
        two = [sems.at[2 * i], sems.at[2 * i + 1]]
        copies += sums(
            ensemble, first + at, at, train, matrix, weight, got, out, buffer, two, length
        )
        at += length
    for copy in copies:
        copy.wait()


def ahead_kernel(last, first, train, matrix, weight, bucket, shared, _, own, final, weight2):
    count = own.shape[0]
    own[...] = scaled(train[:count, :], matrix[...], weight[:count, :])
    rows = pl.ds(last, final.shape[0])
    final[...] = scaled(train[rows, :], matrix[...], weight[rows, :])
    table = jnp.zeros((shared.shape[0] - first, LANES), F32)
    for part in range(3):
        lanes = pl.ds(part * LANES, LANES)
        table = table + shared[first:, lanes].astype(F32)
    weight2[...] = weights_of(bucket[:, :count], table)


def last_kernel(ensemble, first, own, *rest):
    out, buffer, sems = rest[-3:]
    total = own[...].astype(F32)
    for other in rest[: ensemble - 1]:
        total = total + other[...].astype(F32)
    two = [sems.at[0], sems.at[1]]
    for copy in store(out, first, 0, buffer, two, total / ensemble):
        copy.wait()


def both_kernel(ensemble, masks, outers, batches, lengths, me, own, weight2, *rest):
    features, pieces = rest[:batches], rest[batches : batches + len(masks)]
    out, matrix2, buffer, sems = rest[-4:]
    rows = pieces[0].shape[1]
    for mask, piece in zip(masks, pieces):
        for i, outer in enumerate(outers):
            at = lax.bitwise_xor(me[0], mask ^ outer)
            matrix2[aligned(at, rows), :] = piece[i]
    copies, first = [], 0
    for i, (batch, each) in enumerate(zip(features, lengths)):
        rows = pl.ds(first, each)
        total = own[rows, :].astype(F32)
        total = total + scaled(batch[:each, :], matrix2[...], weight2[rows, :]).astype(F32)
        two = [sems.at[2 * i], sems.at[2 * i + 1]]
        copies += store(out, 0, first, buffer, two, total / ensemble)
        first += each
    for copy in copies:
        copy.wait()


def shards(train_feat, test_feat, kernel_inv, bucket_weight, bucket, test_order):
    ensemble, n = lax.axis_size("ckpt"), lax.axis_size("train")
    outer_bits, inner_bits, core_bits = bits_of(n)
    outers = masks_of(outer_bits)
    inners = masks_of(inner_bits + core_bits)
    train = train_feat[0]
    rows, size = train.shape
    count = test_order.shape[0]
    width = count // ensemble
    share = size // n
    unit = rows // 64
    paired = ensemble == 2 and width >= 3 * LANES
    batches = [14, 14] if paired else []
    featured = sum(batches)
    parts = [18, 8, 10] if paired else [32, 32]
    flying = 1 if paired else 2
    table_rows = -(-bucket_weight.shape[1] // 16) * 16

    ckpt = lax.axis_index("ckpt").astype(jnp.int32).reshape(1)
    me = lax.axis_index("train").astype(jnp.int32).reshape(1)
    order = test_order.reshape(len(outers), 1, count // len(outers))
    bucket = bucket.reshape(1, rows)

    sent = [
        shape((part * unit, size))
        for part in batches
    ]
    steps = 2
    own, *features = call(
        functools.partial(start_kernel, steps),
        [shape((2, test_feat.shape[1], size)), *sent],
        (test_feat, kernel_inv, train), [ANY] * 3,
        out_specs=[ANY] * (1 + len(sent)), mib=60,
        scratch=[
            pltpu.VMEM((2, test_feat.shape[1], size), BF16),
            pltpu.VMEM((max(featured, 1) * unit, size), BF16),
            pltpu.SemaphoreType.DMA((2, 3 + steps * len(sent))),
        ],
    )
    features = [lax.ppermute(batch, "ckpt", ahead(1, ensemble)) for batch in features]

    groups = []
    for mask, block in sorted(spread(own, outer_bits, n), key=lambda e: e[0]):
        held = [(mask, block)]
        inner = spread(block, inner_bits, n, mask)[1:]
        held = spread_on(held + inner, core_bits, n)
        groups.append(([m for m, _ in held], [b for _, b in held]))
    weight = call(
        functools.partial(weights_kernel, table_rows), shape((rows, LANES), F32),
        (bucket, bucket_weight), [VMEM] * 2,
    )

    half = 2 * size * size * width
    state = []
    for masks, blocks in groups[:-1]:
        operands = [ckpt, me, order, *blocks, *state]
        after = features[:1] if not state else [weight]
        state = call(
            functools.partial(part_kernel, ensemble, masks),
            [shape((size, size)), shape((count, size))],
            [*operands, *after], [SMEM] * 2 + [VMEM] * (len(operands) - 2) + [ANY] * len(after),
            scratch=[pltpu.VMEM((count // len(outers), size), BF16)],
            aliases={len(operands) - 2: 0, len(operands) - 1: 1} if state else None,
            flops=4 * half, moved=4 * size * size,
        )
    masks, blocks = groups[-1]
    starts = [featured + sum(parts[:q]) for q in range(len(parts))]
    inverse, chosen, test, matrices, shard = call(
        functools.partial(send_transform_kernel, ensemble, masks, share),
        [
            shape((size, size)), shape((count, size)), shape((count // len(outers), size)),
            shape((ensemble - 1, size, width)), shape((share + table_rows, width)),
        ],
        [ckpt, me, order, bucket_weight, *blocks, *state],
        [SMEM] * 2 + [VMEM] * (4 + len(blocks)),
        aliases={4 + len(blocks): 0, 5 + len(blocks): 1},
        flops=3 * half, moved=4 * size * size, mib=12,
    )

    def send(first, part, after):
        got = []
        for k in range(1, ensemble):
            tile = call(
                functools.partial(send_kernel, first * unit, part * unit, k - 1),
                shape((part * unit, width)),
                (train, matrices, weight, *after), [VMEM] * 3 + [ANY] * len(after),
            )
            after = [tile]
            got.append(lax.ppermute(tile, "ckpt", ahead(k, ensemble)))
        return got, after

    received, after = [], []
    if paired:
        shard2 = lax.ppermute(shard, "ckpt", ahead(1, ensemble))
    for q in range(min(flying, len(parts))):
        got, after = send(starts[q], parts[q], after)
        received.append(got)
    if paired:
        piece = call(head_kernel, shape((share, width)), (shard2, *after), [VMEM, ANY])
        after = [piece]

    matrix = call(
        functools.partial(own_transform_kernel, ensemble, masks),
        shape((size, width)), (ckpt, me, order, inverse, chosen, test, *after, *features[1:]),
        [SMEM] * 2 + [VMEM] * 4 + [ANY] * (len(after) + len(features[1:])), flops=3 * half, mib=12,
    )
    if paired:
        got, after = send(starts[flying], parts[flying], after)
        received.append(got)
        column = call(
            functools.partial(stack_kernel, len(outers)), shape((len(outers), share, width)),
            [piece] + [swap(piece, mask, n) for mask in outers[1:]] + [matrix],
            [VMEM] * len(outers) + [ANY],
        )
        for q in range(flying + 1, len(parts)):
            got, after = send(starts[q], parts[q], [column])
            received.append(got)
        own_rows, last_rows, weight2 = call(
            functools.partial(ahead_kernel, starts[-1] * unit, share),
            [
                shape((featured * unit, width)), shape((parts[-1] * unit, width)),
                shape((featured * unit, LANES), F32),
            ],
            (train, matrix, weight, bucket, shard2, column), [VMEM] * 5 + [ANY], mib=16,
        )
        held = [(0, column)]
        for bit in inner_bits:
            held += [(mask ^ bit, swap(b, bit, n)) for mask, b in held]
        held = held[:1] + [
            (mask, call(relay_kernel, shape(b.shape), (b, *received[0], *received[1], own_rows), [VMEM] + [ANY] * 3))
            for mask, b in held[1:]
        ]
        for bit in core_bits:
            held += [(mask ^ bit, swap(b, bit, n)) for mask, b in held]
        pieces = [b for _, b in sorted(held, key=lambda entry: entry[0])]

    out = None

    def put(kernel, part, copies, operands, specs, scratch=()):
        held = [] if out is None else [out]
        return call(
            kernel, shape((rows, width), F32),
            (*operands, *held), specs + [ANY] * len(held),
            out_specs=[ANY],
            scratch=[
                *scratch, pltpu.VMEM((part * unit, width), F32), pltpu.SemaphoreType.DMA((copies,)),
            ],
            aliases={len(operands): 0} if held else None, mib=24,
        )

    together = [[0, 1], [], [2]] if paired else [[q] for q in range(len(parts))]
    for chunks in together:
        part = sum(parts[q] for q in chunks)
        got = [tile for q in chunks for tile in received[q]]
        if paired and not chunks:
            lengths = [part * unit for part in batches]
            out = put(
                functools.partial(both_kernel, ensemble, inners, outers, len(batches), lengths),
                featured, 2 * len(batches), (me, own_rows, weight2, *features, *pieces),
                [SMEM] + [VMEM] * (2 + len(features) + len(pieces)),
                scratch=[pltpu.VMEM((size, width), BF16)],
            )
        elif paired and chunks == together[-1]:
            out = put(
                functools.partial(last_kernel, ensemble, starts[chunks[0]] * unit),
                part, 2, (last_rows, *got), [VMEM] * (1 + len(got)),
            )
        else:
            lengths = [parts[q] * unit for q in chunks]
            out = put(
                functools.partial(sum_kernel, ensemble, starts[chunks[0]] * unit, lengths),
                part, 2 * len(chunks), (train, matrix, weight, *got), [VMEM] * (3 + len(got)),
            )
    return out


def solution(mesh):
    return jax.shard_map(
        shards,
        mesh=mesh,
        in_specs=(
            P("ckpt", "train", None),
            P("ckpt", "train", None),
            P("ckpt", "train", None),
            P("ckpt", None),
            P("train"),
            P(),
        ),
        out_specs=P("train", "ckpt"),
        check_vma=False,
    )
```
